256 devices in a mesh: seg: 16 (over y, z_hi, core), fft: 16 (over x, z_lo).
Axes of the slice: x: 4, y: 4, z: 8 (z_hi: 2, z_lo: 4; z = z_hi * 4 + z_lo), core: 2. Of those that a mesh axis runs over, the one named last changes fastest.
Arguments:
- baseband: bfloat16 [16, 16, 1, 2, 8, 61440], P('seg', 'fft'), may hold values from -6 to 6
- chirp_phase: float32 [16, 128, 16, 256], P('fft'), may hold values from -3.140625 to 3.140625
Outputs:
- filterbank: float32 [16, 15, 16, 128, 256], P('seg', None, 'fft')
The draws below stay inside these ranges and needn't reach their ends.
All inputs are finite; a program needn't handle non-finite values.
Results may differ from the reference program's by a relative error of at most 0.0003.
Values may be sent and summed in bfloat16 or wider, within the bound.
A program may use at most 128 MiB of HBM per device.

```python
import jax
import jax.numpy as jnp
from jax import lax

FFT_LEN = 8388608
CHANNELS = 256
POLS = 1
LOW = 128
SPLIT_H = 256
SEGMENTS = 16
LANES = 16
TAIL = 524288
INNER = 8
OWN_COLS = 61440
EHI = 16
RUN = 128


def block_levels(own_key, shape, shards, least, top_value):
    loudness, own = 1.0, jax.random.fold_in(own_key, 6)
    for position, shards_of in shards:
        heights = jnp.exp(jax.random.uniform(jax.random.fold_in(own, position), (shards_of,), jnp.float32, least / len(shards), top_value / len(shards)))
        loudness = loudness * jnp.repeat(heights, shape[position] // shards_of).reshape([-1 if axis == position else 1 for axis in range(len(shape))])
    return loudness


def noise(stream_key, shape, spread, bound, shards=(), kind=jnp.bfloat16):
    values = spread * jax.random.normal(stream_key, shape, jnp.float32)
    if shards:
        values = values * block_levels(stream_key, shape, shards, -0.22, 0.18)
    return jnp.clip(values, -bound, bound).astype(kind)


def setup_inputs(seed: int = 0) -> dict:
    key_list = jax.random.split(jax.random.key(seed), 3)
    return {
        "baseband": noise(key_list[0], (SEGMENTS, LANES, POLS, 2, INNER, OWN_COLS), 1.0, 6.0, ((0, 16), (1, 16))),
        "chirp_phase": jnp.clip(jax.random.uniform(key_list[1], (LANES, LOW, EHI, SPLIT_H), jnp.float32, -3.140625, 3.140625), -3.140625, 3.140625),
    }


def stream_of(segment_data):
    ordered = jnp.transpose(segment_data.astype(jnp.float32), (1, 2, 4, 3, 0))
    return ordered.reshape(POLS, 2, -1)


def reference(baseband, chirp_phase):
    step_len = FFT_LEN - TAIL
    flat_phase = jnp.transpose(chirp_phase, (1, 3, 2, 0)).reshape(FFT_LEN)
    chirp_turn = lax.complex(jnp.cos(flat_phase), jnp.sin(flat_phase))

    def one_segment(segment):
        own_part = stream_of(lax.dynamic_index_in_dim(baseband, segment, 0, keepdims=False))
        following = jnp.minimum(segment + 1, SEGMENTS - 1).astype(jnp.int32)
        next_part = stream_of(lax.dynamic_index_in_dim(baseband, following, 0, keepdims=False))[:, :, :TAIL]
        next_part = jnp.where(segment + 1 < SEGMENTS, next_part, jnp.zeros_like(next_part))
        window = jnp.concatenate([own_part, next_part], axis=2)
        signal = lax.complex(window[:, 0], window[:, 1])
        spectrum = jnp.fft.fft(signal, axis=-1) * chirp_turn
        series = jnp.fft.ifft(spectrum, axis=-1)[:, :step_len]
        channels = jnp.fft.fft(series.reshape(POLS, -1, CHANNELS), axis=-1)
        detected = jnp.sum(jnp.real(channels) * jnp.real(channels) + jnp.imag(channels) * jnp.imag(channels), axis=0) / CHANNELS
        return detected.reshape(LANES - 1, LANES, RUN, CHANNELS)

    return lax.map(one_segment, jnp.arange(SEGMENTS, dtype=jnp.int32))
```

```python
import functools

import jax
import jax.numpy as jnp
import ml_dtypes
import numpy as np
from jax import lax
from jax.experimental import pallas as pl
from jax.experimental.pallas import tpu as pltpu
from jax.sharding import PartitionSpec as P

FFT_LEN = 8388608
LANES = 16
SEGS = 16
OWN = 61440
TAIL = 4096
COLS = OWN + TAIL
JC = 4
NC = 16 // JC
QC = 4
RQ = 32
KNEE = 4.0
POWER = 20
SHIFT = 2.0**-6.25
TINY = 1e-36

MESH = pl.DeviceIdType.MESH
f32 = jnp.float32
bf16 = jnp.bfloat16


def unit(numerator, modulus, direction):
    angle = (np.asarray(numerator, np.int64) % modulus) * (direction * 2.0 * np.pi / modulus)
    return np.cos(angle), np.sin(angle)


def halves(table):
    table = table.astype(np.float32)
    high = table.astype(ml_dtypes.bfloat16)
    low = (table - high.astype(np.float32)).astype(ml_dtypes.bfloat16)
    return high, low


@functools.lru_cache(maxsize=None)
def tables():
    n = FFT_LEN
    r16, r128, r256 = np.arange(16), np.arange(128), np.arange(256)
    out = {}
    c, s = unit(
        r16[None, :, None] * r16[None, None, :] * (n // 256) + r16[:, None, None] * r16[None, None, :],
        n,
        -1,
    )
    out["s1"] = np.stack([c, s]).astype(np.float32).reshape(2, -1)
    c, s = unit(r16[:, None] * r16[None, :], 256, 1)
    out["s2"] = np.stack([c, s]).astype(np.float32).reshape(2, -1)
    e = r16[:, None] + 16 * r16[None, :]
    ib = 16 * np.arange(8)[:, None] + 128 * r256[None, :]
    c, s = unit(e[:, :, None, None] * ib[None, None], n, -1)
    out["pw"] = np.stack([c, s]).astype(np.float32)
    c, s = unit(r256[:, None] * r256[None, :], 256, -1)
    out["g"] = halves(np.block([[c, s], [-s, c]]))
    res = r16[:, None] + 16 * np.arange(8)[None, :]
    c, s = unit(res[:, :, None] * r256[None, None, :], 32768, -1)
    out["c2"] = np.stack([c, s], axis=1).astype(np.float32)
    src, i = r16[:, None], np.arange(8)[None, :]
    num = (src + 16 * i)[None, None] * r128[None, :, None, None] * (n // 128)
    num = num + src[None, None] * 16 * r16[:, None, None, None]
    c, s = unit(num, n, -1)
    full = np.zeros((16, 2, 128, 16, 2, 8))
    full[:, 0, :, :, 0], full[:, 0, :, :, 1] = c, -s
    full[:, 1, :, :, 0], full[:, 1, :, :, 1] = s, c
    out["a"] = halves(full.reshape(16, 256, 256))
    num = r128[None, :, None] * r128[None, None, :] * (n // 128) + r128[None, :, None] * 16 * r16[:, None, None]
    c, s = unit(num, n, 1)
    out["b"] = halves(np.concatenate([np.concatenate([c, -s], 2), np.concatenate([s, c], 2)], 1))
    c, s = unit(r128[:, None] * r256[None, :], 32768, 1)
    out["base"] = np.stack([c, s]).astype(np.float32)
    c, s = unit(r16[:, None] * r128[None, :], n, 1)
    gl = np.stack([c, s], axis=1).astype(np.float32)
    out["gl"] = np.ascontiguousarray(np.broadcast_to(gl[..., None], gl.shape + (128,)))
    q, par, jj = np.meshgrid(np.arange(QC), np.arange(2), np.arange(RQ), indexing="ij")
    hh = 2 * (RQ * q + jj) + par
    hh = hh.reshape(QC, 2 * RQ)
    c, s = unit(hh[:, :, None] * r256[None, None, :], 256, 1)
    out["h"] = halves(np.concatenate([np.concatenate([c, -s], 2), np.concatenate([s, c], 2)], 1))
    e = r16[:, None] + 16 * r16[None, :]
    c, s = unit(hh.reshape(1, 256, 1) * e[:, None, :], 65536, 1)
    cj = np.zeros((16, 2, 256, 128), np.float32)
    cj[:, 0, :, :16], cj[:, 1, :, :16] = c, s
    out["cj"] = cj
    r = np.arange(256)
    c, s = unit(r[:, None] * r256[None, :], 256, -1)
    out["q"] = halves(np.block([[c, s], [-s, c]]) * 2.0**-27)
    return out


def cmul(ar, ai, br, bi):
    return ar * br - ai * bi, ar * bi + ai * br


def radix4(x, sign):
    (ar, ai), (br, bi), (cr, ci), (dr, di) = x
    pr, pi, mr, mi = ar + cr, ai + ci, ar - cr, ai - ci
    qr, qi, nr, ni = br + dr, bi + di, br - dr, bi - di
    if sign > 0:
        ur, ui = -ni, nr
        return [(pr + qr, pi + qi), (mr - ni, mi + nr), (pr - qr, pi - qi), (mr + ni, mi - nr)]
    return [(pr + qr, pi + qi), (mr + ni, mi - nr), (pr - qr, pi - qi), (mr - ni, mi + nr)]


def turn(x, power, sign):
    xr, xi = x
    power = power % 16
    if power == 0:
        return x
    if power == 4:
        return (-xi, xr) if sign > 0 else (xi, -xr)
    root = float(np.sqrt(0.5))
    if power == 2:
        return ((xr - xi) * root, (xr + xi) * root) if sign > 0 else ((xr + xi) * root, (xi - xr) * root)
    if power == 6:
        return ((-xr - xi) * root, (xr - xi) * root) if sign > 0 else ((xi - xr) * root, (-xr - xi) * root)
    c = float(np.cos(2 * np.pi * power / 16))
    s = float(sign * np.sin(2 * np.pi * power / 16))
    return (xr * c - xi * s, xr * s + xi * c)


def radix16(x, sign):
    inner = [radix4([x[4 * n1 + n2] for n1 in range(4)], sign) for n2 in range(4)]
    out = [None] * 16
    for k1 in range(4):
        column = radix4([turn(inner[n2][k1], n2 * k1, sign) for n2 in range(4)], sign)
        for k2 in range(4):
            out[k1 + 4 * k2] = column[k2]
    return out


def split(x):
    high = x.astype(bf16)
    return high, (x - high.astype(f32)).astype(bf16)


def dot(a, b):
    return lax.dot_general(a, b, (((1,), (0,)), ((), ())), preferred_element_type=f32)


def dot3(ah, al, bh, bl):
    return dot(ah, bh) + dot(al, bh) + dot(ah, bl)


def encode(x, inverse):
    a = jnp.abs(x) * inverse
    v = a * a + 1.0
    w = (a + v * lax.rsqrt(v)) * SHIFT
    w2 = w * w
    w4 = w2 * w2
    w8 = w4 * w4
    y = (w8 * w8) * w4
    return jnp.where(x < 0, -y, y)


def decode(y, half_scale):
    t = jnp.log(jnp.abs(y)) * (1.0 / POWER) + float(-np.log(SHIFT))
    w = jnp.exp(t)
    a = (w - jnp.exp(-t)) * half_scale
    return jnp.where(y < 0, -a, a)


def cos_sin(x):
    y = x * 0.5
    z = y * y
    s = 1.0 / 6227020800.0
    for factor in (-1.0 / 39916800.0, 1.0 / 362880.0, -1.0 / 5040.0, 1.0 / 120.0, -1.0 / 6.0, 1.0):
        s = s * z + factor
    s = s * y
    c = 1.0 / 479001600.0
    for factor in (-1.0 / 3628800.0, 1.0 / 40320.0, -1.0 / 720.0, 1.0 / 24.0, -0.5, 1.0):
        c = c * z + factor
    return 1.0 - 2.0 * s * s, 2.0 * s * c


def aligned(index, size):
    return pl.ds(pl.multiple_of(index * size, size), size)


def kernel(
    x_hbm, chirp_hbm, s1_ref, s2_ref, pw_hbm, gh_hbm, gl_hbm, c2_hbm, ah_hbm, al_hbm, bh_hbm, bl_hbm,
    base_hbm, lane_hbm, hh_hbm, hl_hbm, cj_hbm, qh_hbm, ql_hbm,
    out_hbm,
    x_v, d_v, pw_v, lhs_h, lhs_l, y_v, send1, recv1, send2, recv2, scale1_out, scale1, scale2_out, scale2,
    gh_v, gl_v, c2_v, ah_v, al_v, bh_v, bl_v, base_v, lane_v, hh_v, hl_v, cj_v, qh_v, ql_v,
    chirp_v, turn_v, wt_h, wt_l, u_v, v_v, z_v, xl_v, stage,
    load_sem, chirp_sem, tail_sems, scale_sems, send_sem1, recv_sem1, own_sem1, send_sem2, recv_sem2, own_sem2,
    out_sem,
):
    lane = lax.axis_index("fft")
    seg = lax.axis_index("seg")
    peer = lambda s: lax.rem(lane + s, LANES)

    def load(source, target, index):
        copy = pltpu.make_async_copy(source, target, load_sem.at[index])
        copy.start()
        return copy

    load_x = load(x_hbm, x_v.at[:, pl.ds(0, OWN)], 0)

    barrier = pltpu.get_barrier_semaphore()
    before, after = lax.rem(seg + SEGS - 1, SEGS), lax.rem(seg + 1, SEGS)

    def greet(s, carry):
        pl.semaphore_signal(barrier, inc=1, device_id={"fft": peer(s)}, device_id_type=MESH)
        return carry

    lax.fori_loop(1, LANES, greet, 0)
    pl.semaphore_signal(barrier, inc=1, device_id={"seg": before}, device_id_type=MESH)
    pl.semaphore_signal(barrier, inc=1, device_id={"seg": after}, device_id_type=MESH)

    load_pw = load(pw_hbm, pw_v, 1)
    load_g = [load(gh_hbm, gh_v, 2), load(gl_hbm, gl_v, 3), load(c2_hbm.at[lane], c2_v, 4)]

    pl.semaphore_wait(barrier, LANES + 1)
    tail = pltpu.make_async_remote_copy(
        src_ref=x_hbm.at[:, pl.ds(0, TAIL)],
        dst_ref=x_v.at[:, pl.ds(OWN, TAIL)],
        send_sem=tail_sems.at[0],
        recv_sem=tail_sems.at[1],
        device_id={"seg": before},
        device_id_type=MESH,
    )
    tail.start()
    load_x.wait()

    late = [
        load(ah_hbm, ah_v, 5), load(al_hbm, al_v, 6), load(bh_hbm, bh_v, 7), load(bl_hbm, bl_v, 8),
        load(base_hbm, base_v, 9), load(lane_hbm.at[lane], lane_v, 10), load(hh_hbm, hh_v, 11),
        load(hl_hbm, hl_v, 12), load(cj_hbm.at[lane], cj_v, 13), load(qh_hbm, qh_v, 14), load(ql_hbm, ql_v, 15),
    ]

    def chirp_copy(j):
        return pltpu.make_async_copy(chirp_hbm.at[:, j, :], chirp_v.at[j], chirp_sem.at[j])

    def chirp_start(j, carry):
        chirp_copy(j).start()
        return carry

    lax.fori_loop(0, 16, chirp_start, 0)

    tail.wait()

    @pl.when(seg == SEGS - 1)
    def _():
        x_v[:, pl.ds(OWN, TAIL)] = jnp.zeros((16, TAIL), bf16)

    def first_pass(t, energy):
        a_lo, half = t // 2, lax.rem(t, 2)
        x = []
        for a_hi in range(16):
            block = x_v[:, aligned((16 * a_hi + a_lo) * 2 + half, 128)].astype(f32)
            re, im = block[:8], block[8:]
            energy = energy + (re * re + im * im)
            x.append((re, im))
        x = radix16(x, -1)
        for e_lo in range(16):
            where = lane * 256 + a_lo * 16 + e_lo
            re, im = cmul(*x[e_lo], s1_ref[0, where], s1_ref[1, where])
            d_v[0, e_lo, a_lo, :, aligned(half, 128)] = re
            d_v[1, e_lo, a_lo, :, aligned(half, 128)] = im
        return energy

    energy = lax.fori_loop(0, 32, first_pass, jnp.zeros((8, 128), f32))

    def scale_of(energy):
        total = jnp.sum(jnp.sum(energy, axis=1, keepdims=True), axis=0, keepdims=True)
        mean = jnp.maximum(jnp.broadcast_to(total, (8, 128)), TINY)
        return mean * lax.rsqrt(mean) * (1.0 / KNEE)

    def send_scale(value, out_ref, in_ref, sems):
        out_ref[...] = value
        in_ref[lane] = value

        def send(s, carry):
            pltpu.make_async_remote_copy(
                src_ref=out_ref, dst_ref=in_ref.at[lane], send_sem=sems.at[0], recv_sem=sems.at[1],
                device_id={"fft": peer(s)}, device_id_type=MESH,
            ).start()
            return carry

        lax.fori_loop(1, LANES, send, 0)

    def wait_total(ref, sem):
        pltpu.make_async_copy(ref, ref, sem).wait()

    my_scale = scale_of(energy * 0.125)
    send_scale(my_scale, scale1_out, scale1, scale_sems.at[0])
    inverse = 1.0 / my_scale
    inverse = jnp.concatenate([inverse, inverse], axis=1)

    load_pw.wait()

    def second_pass(t, carry):
        e_lo, half = t // 2, lax.rem(t, 2)
        cols = aligned(half, 128)
        x = [(d_v[0, e_lo, a_lo, :, cols], d_v[1, e_lo, a_lo, :, cols]) for a_lo in range(16)]
        x = radix16(x, -1)
        for e_hi in range(16):
            re, im = cmul(*x[e_hi], pw_v[0, e_lo, e_hi, :, cols], pw_v[1, e_lo, e_hi, :, cols])
            d_v[0, e_lo, e_hi, :, cols] = re
            d_v[1, e_lo, e_hi, :, cols] = im
        return carry

    lax.fori_loop(0, 32, second_pass, 0)

    for copy in load_g:
        copy.wait()

    def chunk1(ref, jc, s):
        return ref.at[peer(s), pl.ds(jc * JC, JC)]

    def landing1(jc, source):
        return recv1.at[pl.ds(jc * JC, JC), source]

    rows = JC * 8

    def transform_b(t, carry):
        jc, half = t // 2, lax.rem(t, 2)
        for u in range(8):
            dest = peer(half * 8 + 1 + u)
            re = d_v[0, dest, pl.ds(jc * JC, JC)].reshape(rows, 256)
            im = d_v[1, dest, pl.ds(jc * JC, JC)].reshape(rows, 256)
            high, low = split(jnp.concatenate([re, im], axis=1))
            lhs_h[pl.ds(u * rows, rows), :] = high
            lhs_l[pl.ds(u * rows, rows), :] = low
        y_v[...] = dot3(lhs_h[...], lhs_l[...], gh_v[...], gl_v[...])
        cr, ci = c2_v[0][None], c2_v[1][None]
        for u in range(8):
            s = half * 8 + 1 + u
            block = y_v[pl.ds(u * rows, rows), :]
            re = block[:, :256].reshape(JC, 8, 256)
            im = block[:, 256:].reshape(JC, 8, 256)
            re, im = cmul(re, im, cr, ci)
            coded = jnp.concatenate([encode(re, inverse[None]), encode(im, inverse[None])], axis=1)
            send1[peer(s), pl.ds(jc * JC, JC)] = coded.astype(bf16)

            def remote():
                pltpu.make_async_remote_copy(
                    src_ref=chunk1(send1, jc, s), dst_ref=landing1(jc, lane),
                    send_sem=send_sem1, recv_sem=recv_sem1.at[jc],
                    device_id={"fft": peer(s)}, device_id_type=MESH,
                ).start()

            if u < 7:
                remote()
            else:
                pl.when(half == 0)(remote)

                @pl.when(half == 1)
                def _():
                    pltpu.make_async_copy(chunk1(send1, jc, s), landing1(jc, lane), own_sem1.at[jc]).start()

        return carry

    lax.fori_loop(0, 2 * NC, transform_b, 0)

    def response(j, carry):
        chirp_copy(j).wait()
        c, s = cos_sin(chirp_v[j])
        turn_v[0, j] = c
        turn_v[1, j] = s
        return carry

    lax.fori_loop(0, 16, response, 0)
    for copy in late:
        copy.wait()
    for part in range(2):
        cols = pl.ds(part * 128, 128)
        re, im = cmul(base_v[0, :, cols], base_v[1, :, cols], lane_v[0], lane_v[1])
        base_v[0, :, cols] = re
        base_v[1, :, cols] = im

    wait_total(scale1.at[pl.ds(0, LANES - 1)], scale_sems.at[0, 1])

    def middle(j, energy):
        half_scale = (scale1[...] * 0.5)[:, 0:1, :]
        half_scale = jnp.concatenate([half_scale, half_scale], axis=2)
        z = decode(recv1[j].astype(f32), half_scale).reshape(256, 256)
        zh, zl = split(z)
        o = dot3(ah_v[j], al_v[j], zh, zl)
        re, im = cmul(o[:128], o[128:], turn_v[0, j], turn_v[1, j])
        ph, pll = split(jnp.concatenate([re, im], axis=0))
        o = dot3(bh_v[j], bl_v[j], ph, pll)
        re, im = cmul(o[:128], o[128:], base_v[0], base_v[1])
        power = re * re + im * im
        energy = energy + jnp.sum(power.reshape(16, 8, 256), axis=0)
        both = jnp.concatenate([re.T, im.T], axis=0)
        high, low = split(both)
        wt_h[:, aligned(j, 128)] = high
        wt_l[:, aligned(j, 128)] = low
        return energy

    def middle_chunk(jc, energy):
        wait_total(recv1.at[pl.ds(jc * JC, JC), pl.ds(0, LANES - 1)], recv_sem1.at[jc])
        wait_total(landing1(jc, lane), own_sem1.at[jc])
        return lax.fori_loop(jc * JC, jc * JC + JC, middle, energy)

    energy = lax.fori_loop(0, NC, middle_chunk, jnp.zeros((8, 256), f32))
    my_scale = scale_of((energy[:, :128] + energy[:, 128:]) * (1.0 / 128.0))
    send_scale(my_scale, scale2_out, scale2, scale_sems.at[1])
    inverse2 = (1.0 / my_scale)[0:1, :]

    def post(q, carry):
        def columns(block, inner):
            cols = aligned(block, 512)
            u_v[:, cols] = dot3(hh_v[q], hl_v[q], wt_h[:, cols], wt_l[:, cols])
            return inner

        lax.fori_loop(0, 4, columns, 0)

        def rows_of(rt, inner):
            top = aligned(rt, 8)
            low = pl.ds(pl.multiple_of(2 * RQ + rt * 8, 8), 8)
            table = pl.ds(pl.multiple_of(q * 2 * RQ + rt * 8, 8), 8)
            tr, ti = cj_v[0, table, :], cj_v[1, table, :]
            x = []
            for j in range(16):
                cols = pl.ds(j * 128, 128)
                x.append(cmul(u_v[top, cols], u_v[low, cols], tr[:, j : j + 1], ti[:, j : j + 1]))
            x = radix16(x, 1)
            for l in range(16):
                re, im = cmul(*x[l], s2_ref[0, lane * 16 + l], s2_ref[1, lane * 16 + l])
                v_v[l, 0, top, :] = re
                v_v[l, 1, top, :] = im
            return inner

        lax.fori_loop(0, 2 * RQ // 8, rows_of, 0)

        def code(s, inner):
            dest = peer(s)
            send2[dest, q] = encode(v_v[dest], inverse2[None]).astype(bf16)

            @pl.when(s < LANES)
            def _():
                pltpu.make_async_remote_copy(
                    src_ref=send2.at[dest, q], dst_ref=recv2.at[q, lane],
                    send_sem=send_sem2, recv_sem=recv_sem2.at[q],
                    device_id={"fft": dest}, device_id_type=MESH,
                ).start()

            @pl.when(s == LANES)
            def _():
                pltpu.make_async_copy(send2.at[dest, q], recv2.at[q, lane], own_sem2.at[q]).start()

            return inner

        return lax.fori_loop(1, LANES + 1, code, carry)

    lax.fori_loop(0, QC, post, 0)

    wait_total(scale2.at[pl.ds(0, LANES - 1)], scale_sems.at[1, 1])

    def out_copy(q):
        return pltpu.make_async_copy(stage.at[lax.rem(q, 2)], out_hbm.at[:, pl.ds(q * RQ, RQ), :], out_sem.at[q])

    def final(q, carry):
        wait_total(recv2.at[q, pl.ds(0, LANES - 1)], recv_sem2.at[q])
        wait_total(recv2.at[q, lane], own_sem2.at[q])

        def undo(source, inner):
            half_scale = (scale2[source] * 0.5)[0:1, :]
            z_v[source] = decode(recv2[q, source].astype(f32), half_scale[None])
            return inner

        lax.fori_loop(0, LANES, undo, 0)

        def rows_of(rt, inner):
            top = aligned(rt, 8)
            par, jt = rt // (RQ // 8), lax.rem(rt, RQ // 8)
            x = radix16([(z_v[s, 0, top, :], z_v[s, 1, top, :]) for s in range(16)], 1)
            for t in range(15):
                where = pl.ds(pl.multiple_of(t * RQ + jt * 8, 8), 8)
                xl_v[where, aligned(par, 128)] = x[t][0]
                xl_v[where, aligned(par + 2, 128)] = x[t][1]
            return inner

        lax.fori_loop(0, 2 * RQ // 8, rows_of, 0)

        @pl.when(q >= 2)
        def _():
            out_copy(q - 2).wait()

        def channels(block, inner):
            high, low = split(xl_v[aligned(block, 5 * RQ), :])
            y = dot3(high, low, qh_v[...], ql_v[...])
            re, im = y[:, :256], y[:, 256:]
            stage[lax.rem(q, 2), pl.ds(block * 5, 5)] = (re * re + im * im).reshape(5, RQ, 256)
            return inner

        lax.fori_loop(0, 3, channels, 0)
        out_copy(q).start()
        return carry

    lax.fori_loop(0, QC, final, 0)
    out_copy(QC - 2).wait()
    out_copy(QC - 1).wait()

    wait_total(scale1.at[pl.ds(0, LANES - 1)], scale_sems.at[0, 0])
    wait_total(scale2.at[pl.ds(0, LANES - 1)], scale_sems.at[1, 0])
    wait_total(send1.at[pl.ds(0, LANES - 1)], send_sem1)
    wait_total(send2.at[pl.ds(0, LANES - 1)], send_sem2)


def on_device(baseband, chirp_phase):
    t = tables()
    constants = [
        t["s1"], t["s2"], t["pw"], *t["g"], t["c2"], *t["a"], *t["b"], t["base"], t["gl"], *t["h"], t["cj"], *t["q"],
    ]
    constants = [jnp.asarray(c) for c in constants]
    anywhere = pl.BlockSpec(memory_space=pl.ANY)
    scalars = pl.BlockSpec(memory_space=pltpu.SMEM)
    v = lambda shape, kind=f32: pltpu.VMEM(shape, kind)
    dma = pltpu.SemaphoreType.DMA
    out = pl.pallas_call(
        kernel,
        out_shape=jax.ShapeDtypeStruct((15, 128, 256), f32),
        in_specs=[anywhere, anywhere, scalars, scalars] + [anywhere] * (len(constants) - 2),
        out_specs=anywhere,
        scratch_shapes=[
            v((16, COLS), bf16), v((2, 16, 16, 8, 256)), v((2, 16, 16, 8, 256)),
            v((JC * 64, 512), bf16), v((JC * 64, 512), bf16), v((JC * 64, 512)),
            v((16, 16, 16, 256), bf16), v((16, 16, 16, 256), bf16),
            v((16, QC, 2, 2 * RQ, 128), bf16), v((QC, 16, 2, 2 * RQ, 128), bf16),
            v((8, 128)), v((16, 8, 128)), v((8, 128)), v((16, 8, 128)),
            v((512, 512), bf16), v((512, 512), bf16), v((2, 8, 256)),
            v((16, 256, 256), bf16), v((16, 256, 256), bf16), v((16, 256, 256), bf16), v((16, 256, 256), bf16),
            v((2, 128, 256)), v((2, 128, 128)),
            v((QC, 4 * RQ, 512), bf16), v((QC, 4 * RQ, 512), bf16), v((2, 256, 128)),
            v((512, 512), bf16), v((512, 512), bf16),
            v((16, 128, 256)), v((2, 16, 128, 256)),
            v((512, 2048), bf16), v((512, 2048), bf16), v((4 * RQ, 2048)),
            v((16, 2, 2 * RQ, 128)), v((16, 2, 2 * RQ, 128)), v((15 * RQ, 512)), v((2, 15, RQ, 256)),
            dma((16,)), dma((16,)), dma((2,)), dma((2, 2)), dma, dma((NC,)), dma((NC,)), dma, dma((QC,)),
            dma((QC,)), dma((QC,)),
        ],
        compiler_params=pltpu.CompilerParams(
            collective_id=0, has_side_effects=True, vmem_limit_bytes=60 * 1024 * 1024
        ),
        name="dedisperse",
    )(baseband.reshape(16, OWN), chirp_phase.reshape(128, 16, 256), *constants)
    return out.reshape(1, 15, 1, 128, 256)


def solution(mesh):
    return jax.shard_map(
        on_device,
        mesh=mesh,
        in_specs=(P("seg", "fft", None, None, None, None), P("fft", None, None, None)),
        out_specs=P("seg", None, "fft", None, None),
        check_vma=False,
    )
```

```python
import functools

import jax
import jax.numpy as jnp
import ml_dtypes
import numpy as np
from jax import lax
from jax.experimental import pallas as pl
from jax.experimental.pallas import tpu as pltpu
from jax.sharding import PartitionSpec as P

FFT_LEN = 8388608
LANES = 16
SEGS = 16
OWN = 61440
TAIL = 4096
COLS = OWN + TAIL
JC = 2
NC = 16 // JC
QC = 8
RQ = 16
KNEE = 4.0
POWER = 20
SHIFT = 2.0**-6.25
TINY = 1e-36

MESH = pl.DeviceIdType.MESH
f32 = jnp.float32
bf16 = jnp.bfloat16


def unit(numerator, modulus, direction):
    angle = (np.asarray(numerator, np.int64) % modulus) * (direction * 2.0 * np.pi / modulus)
    return np.cos(angle), np.sin(angle)


def halves(table):
    table = table.astype(np.float32)
    high = table.astype(ml_dtypes.bfloat16)
    low = (table - high.astype(np.float32)).astype(ml_dtypes.bfloat16)
    return high, low


@functools.lru_cache(maxsize=None)
def tables():
    n = FFT_LEN
    r16, r128, r256 = np.arange(16), np.arange(128), np.arange(256)
    out = {}
    c, s = unit(
        r16[None, :, None] * r16[None, None, :] * (n // 256) + r16[:, None, None] * r16[None, None, :],
        n,
        -1,
    )
    out["s1"] = np.stack([c, s]).astype(np.float32).reshape(2, -1)
    c, s = unit(r16[:, None] * r16[None, :], 256, 1)
    out["s2"] = np.stack([c, s]).astype(np.float32).reshape(2, -1)
    e = r16[:, None] + 16 * r16[None, :]
    ib = 16 * np.arange(8)[:, None] + 128 * r256[None, :]
    c, s = unit(e[:, :, None, None] * ib[None, None], n, -1)
    out["pw"] = np.stack([c, s]).astype(np.float32)
    c, s = unit(r256[:, None] * r256[None, :], 256, -1)
    out["g"] = halves(np.block([[c, s], [-s, c]]))
    res = r16[:, None] + 16 * np.arange(8)[None, :]
    c, s = unit(res[:, :, None] * r256[None, None, :], 32768, -1)
    out["c2"] = np.stack([c, s], axis=1).astype(np.float32)
    src, i = r16[:, None], np.arange(8)[None, :]
    num = (src + 16 * i)[None, None] * r128[None, :, None, None] * (n // 128)
    num = num + src[None, None] * 16 * r16[:, None, None, None]
    c, s = unit(num, n, -1)
    full = np.zeros((16, 2, 128, 16, 2, 8))
    full[:, 0, :, :, 0], full[:, 0, :, :, 1] = c, -s
    full[:, 1, :, :, 0], full[:, 1, :, :, 1] = s, c
    out["a"] = halves(full.reshape(16, 256, 256))
    num = r128[None, :, None] * r128[None, None, :] * (n // 128) + r128[None, :, None] * 16 * r16[:, None, None]
    c, s = unit(num, n, 1)
    out["b"] = halves(np.concatenate([np.concatenate([c, -s], 2), np.concatenate([s, c], 2)], 1))
    c, s = unit(r128[:, None] * r256[None, :], 32768, 1)
    out["base"] = np.stack([c, s]).astype(np.float32)
    c, s = unit(r16[:, None] * r128[None, :], n, 1)
    gl = np.stack([c, s], axis=1).astype(np.float32)
    out["gl"] = np.ascontiguousarray(np.broadcast_to(gl[..., None], gl.shape + (128,)))
    q, par, jj = np.meshgrid(np.arange(QC), np.arange(2), np.arange(RQ), indexing="ij")
    hh = 2 * (RQ * q + jj) + par
    hh = hh.reshape(QC, 2 * RQ)
    c, s = unit(hh[:, :, None] * r256[None, None, :], 256, 1)
    both = np.concatenate([np.concatenate([c, -s], 2), np.concatenate([s, c], 2)], 1)
    out["h"] = halves(both.reshape(512, 512))
    e = r16[:, None] + 16 * r16[None, :]
    c, s = unit(hh.reshape(1, 256, 1) * e[:, None, :], 65536, 1)
    cj = np.zeros((16, 2, 256, 128), np.float32)
    cj[:, 0, :, :16], cj[:, 1, :, :16] = c, s
    out["cj"] = cj
    r = np.arange(256)
    c, s = unit(r[:, None] * r256[None, :], 256, -1)
    out["q"] = halves(np.block([[c, s], [-s, c]]) * 2.0**-27)
    return out


def cmul(ar, ai, br, bi):
    return ar * br - ai * bi, ar * bi + ai * br


def radix4(x, sign):
    (ar, ai), (br, bi), (cr, ci), (dr, di) = x
    pr, pi, mr, mi = ar + cr, ai + ci, ar - cr, ai - ci
    qr, qi, nr, ni = br + dr, bi + di, br - dr, bi - di
    if sign > 0:
        ur, ui = -ni, nr
        return [(pr + qr, pi + qi), (mr - ni, mi + nr), (pr - qr, pi - qi), (mr + ni, mi - nr)]
    return [(pr + qr, pi + qi), (mr + ni, mi - nr), (pr - qr, pi - qi), (mr - ni, mi + nr)]


def turn(x, power, sign):
    xr, xi = x
    power = power % 16
    if power == 0:
        return x
    if power == 4:
        return (-xi, xr) if sign > 0 else (xi, -xr)
    root = float(np.sqrt(0.5))
    if power == 2:
        return ((xr - xi) * root, (xr + xi) * root) if sign > 0 else ((xr + xi) * root, (xi - xr) * root)
    if power == 6:
        return ((-xr - xi) * root, (xr - xi) * root) if sign > 0 else ((xi - xr) * root, (-xr - xi) * root)
    c = float(np.cos(2 * np.pi * power / 16))
    s = float(sign * np.sin(2 * np.pi * power / 16))
    return (xr * c - xi * s, xr * s + xi * c)


def radix16(x, sign):
    inner = [radix4([x[4 * n1 + n2] for n1 in range(4)], sign) for n2 in range(4)]
    out = [None] * 16
    for k1 in range(4):
        column = radix4([turn(inner[n2][k1], n2 * k1, sign) for n2 in range(4)], sign)
        for k2 in range(4):
            out[k1 + 4 * k2] = column[k2]
    return out


def split(x):
    high = x.astype(bf16)
    return high, (x - high.astype(f32)).astype(bf16)


def dot(a, b):
    return lax.dot_general(a, b, (((1,), (0,)), ((), ())), preferred_element_type=f32)


def dot3(ah, al, bh, bl):
    return dot(ah, bh) + dot(al, bh) + dot(ah, bl)


def encode(x, inverse):
    a = jnp.abs(x) * inverse
    v = a * a + 1.0
    w = (a + v * lax.rsqrt(v)) * SHIFT
    w2 = w * w
    w4 = w2 * w2
    w8 = w4 * w4
    y = (w8 * w8) * w4
    return jnp.where(x < 0, -y, y)


def decode(y, half_scale):
    t = jnp.log(jnp.abs(y)) * (1.0 / POWER) + float(-np.log(SHIFT))
    w = jnp.exp(t)
    a = (w - jnp.exp(-t)) * half_scale
    return jnp.where(y < 0, -a, a)


def cos_sin(x):
    y = x * 0.5
    z = y * y
    s = 1.0 / 6227020800.0
    for factor in (-1.0 / 39916800.0, 1.0 / 362880.0, -1.0 / 5040.0, 1.0 / 120.0, -1.0 / 6.0, 1.0):
        s = s * z + factor
    s = s * y
    c = 1.0 / 479001600.0
    for factor in (-1.0 / 3628800.0, 1.0 / 40320.0, -1.0 / 720.0, 1.0 / 24.0, -0.5, 1.0):
        c = c * z + factor
    return 1.0 - 2.0 * s * s, 2.0 * s * c


def aligned(index, size):
    return pl.ds(pl.multiple_of(index * size, size), size)


def kernel(
    x_hbm, chirp_hbm, s1_ref, s2_ref, pw_hbm, gh_hbm, gl_hbm, c2_hbm, ah_hbm, al_hbm, bh_hbm, bl_hbm,
    base_hbm, lane_hbm, hh_hbm, hl_hbm, cj_hbm, qh_hbm, ql_hbm,
    out_hbm,
    x_v, d_v, pw_v, lhs_h, lhs_l, y_v, send1, recv1, send2, recv2, scale1_out, scale1, scale2_out, scale2,
    gh_v, gl_v, c2_v, ah_v, al_v, bh_v, bl_v, base_v, lane_v, hh_v, hl_v, cj_v, qh_v, ql_v,
    chirp_v, turn_v, u_v, v_v, z_v, xl_v, stage,
    load_sem, chirp_sem, head_sems, scale_sems, send_sem1, recv_sem1, own_sem1, send_sem2, recv_sem2, own_sem2,
    out_sem,
):
    lane = lax.axis_index("fft")
    seg = lax.axis_index("seg")
    lane_x, lane_z = lane // 4, lax.rem(lane, 4)

    def peer(turn_index):
        step_z, step_x = (2, 1, 3, 0)[turn_index // 4], (turn_index + 1) % 4
        return lax.rem(lane_x + step_x, 4) * 4 + lax.rem(lane_z + step_z, 4)

    before, after = lax.rem(seg + SEGS - 1, SEGS), lax.rem(seg + 1, SEGS)

    def load(source, target, index):
        copy = pltpu.make_async_copy(source, target, load_sem.at[index])
        copy.start()
        return copy

    load_x = load(x_hbm, x_v.at[:, pl.ds(0, OWN)], 0)

    barrier = pltpu.get_barrier_semaphore()

    @pl.when(seg < SEGS - 1)
    def _():
        pl.semaphore_signal(barrier, inc=1, device_id={"seg": after}, device_id_type=MESH)

    for s in range(LANES - 1):
        pl.semaphore_signal(barrier, inc=1, device_id={"fft": peer(s)}, device_id_type=MESH)
    load_pw = load(pw_hbm, pw_v, 1)
    load_g = [load(gh_hbm, gh_v, 2), load(gl_hbm, gl_v, 3), load(c2_hbm.at[lane], c2_v, 4)]
    head = pltpu.make_async_remote_copy(
        src_ref=x_hbm.at[:, pl.ds(0, TAIL)], dst_ref=x_v.at[:, pl.ds(OWN, TAIL)],
        send_sem=head_sems.at[0], recv_sem=head_sems.at[1],
        device_id={"seg": before}, device_id_type=MESH,
    )

    @pl.when(seg > 0)
    def _():
        pl.semaphore_wait(barrier, LANES)
        head.start()

    @pl.when(seg == 0)
    def _():
        pl.semaphore_wait(barrier, LANES - 1)

    load_x.wait()

    @pl.when(seg < SEGS - 1)
    def _():
        head.wait_recv()

    @pl.when(seg == SEGS - 1)
    def _():
        x_v[:, pl.ds(OWN, TAIL)] = jnp.zeros((16, TAIL), bf16)

    late = [
        load(ah_hbm, ah_v, 5), load(al_hbm, al_v, 6), load(bh_hbm, bh_v, 7), load(bl_hbm, bl_v, 8),
        load(base_hbm, base_v, 9), load(lane_hbm.at[lane], lane_v, 10), load(hh_hbm, hh_v, 11),
        load(hl_hbm, hl_v, 12), load(cj_hbm.at[lane], cj_v, 13), load(qh_hbm, qh_v, 14), load(ql_hbm, ql_v, 15),
    ]

    def chirp_copy(j):
        return pltpu.make_async_copy(chirp_hbm.at[:, j, :], chirp_v.at[j], chirp_sem.at[j])

    def chirp_start(j, carry):
        chirp_copy(j).start()
        return carry

    lax.fori_loop(0, 16, chirp_start, 0)

    def first_pass(t, energy):
        a_lo, half = t // 2, lax.rem(t, 2)
        x = []
        for a_hi in range(16):
            block = x_v[:, aligned((16 * a_hi + a_lo) * 2 + half, 128)].astype(f32)
            re, im = block[:8], block[8:]
            energy = energy + (re * re + im * im)
            x.append((re, im))
        x = radix16(x, -1)
        for e_lo in range(16):
            where = lane * 256 + a_lo * 16 + e_lo
            re, im = cmul(*x[e_lo], s1_ref[0, where], s1_ref[1, where])
            d_v[0, e_lo, a_lo, :, aligned(half, 128)] = re
            d_v[1, e_lo, a_lo, :, aligned(half, 128)] = im
        return energy

    energy = lax.fori_loop(0, 32, first_pass, jnp.zeros((8, 128), f32))

    def scale_of(energy):
        total = jnp.sum(jnp.sum(energy, axis=1, keepdims=True), axis=0, keepdims=True)
        mean = jnp.maximum(jnp.broadcast_to(total, (8, 128)), TINY)
        return mean * lax.rsqrt(mean) * (1.0 / KNEE)

    def send_scale(value, out_ref, in_ref, sems):
        out_ref[...] = value
        in_ref[lane] = value

        for s in range(LANES - 1):
            pltpu.make_async_remote_copy(
                src_ref=out_ref, dst_ref=in_ref.at[lane], send_sem=sems.at[0], recv_sem=sems.at[1],
                device_id={"fft": peer(s)}, device_id_type=MESH,
            ).start()

    def wait_total(ref, sem):
        pltpu.make_async_copy(ref, ref, sem).wait()

    my_scale = scale_of(energy * 0.125)
    inverse = 1.0 / my_scale
    inverse = jnp.concatenate([inverse, inverse], axis=1)

    load_pw.wait()

    def second_pass(t, carry):
        e_lo, half = t // 2, lax.rem(t, 2)
        cols = aligned(half, 128)
        x = [(d_v[0, e_lo, a_lo, :, cols], d_v[1, e_lo, a_lo, :, cols]) for a_lo in range(16)]
        x = radix16(x, -1)
        for e_hi in range(16):
            re, im = cmul(*x[e_hi], pw_v[0, e_lo, e_hi, :, cols], pw_v[1, e_lo, e_hi, :, cols])
            d_v[0, e_lo, e_hi, :, cols] = re
            d_v[1, e_lo, e_hi, :, cols] = im
        return carry

    lax.fori_loop(0, 32, second_pass, 0)

    for copy in load_g:
        copy.wait()
    send_scale(my_scale, scale1_out, scale1, scale_sems.at[0])

    def chunk1(ref, jc, s):
        return ref.at[peer(s), pl.ds(jc * JC, JC)]

    def landing1(jc, source):
        return recv1.at[pl.ds(jc * JC, JC), source]

    rows = JC * 8

    def transform_b(jc, carry):
        for u in range(LANES):
            dest = peer(u)
            re = d_v[0, dest, pl.ds(jc * JC, JC)].reshape(rows, 256)
            im = d_v[1, dest, pl.ds(jc * JC, JC)].reshape(rows, 256)
            high, low = split(jnp.concatenate([re, im], axis=1))
            lhs_h[pl.ds(u * rows, rows), :] = high
            lhs_l[pl.ds(u * rows, rows), :] = low
        y_v[...] = dot3(lhs_h[...], lhs_l[...], gh_v[...], gl_v[...])
        cr, ci = c2_v[0][None], c2_v[1][None]
        for u in range(LANES):
            dest = peer(u)
            block = y_v[pl.ds(u * rows, rows), :]
            re = block[:, :256].reshape(JC, 8, 256)
            im = block[:, 256:].reshape(JC, 8, 256)
            re, im = cmul(re, im, cr, ci)
            coded = jnp.concatenate([encode(re, inverse[None]), encode(im, inverse[None])], axis=1)
            send1[dest, pl.ds(jc * JC, JC)] = coded.astype(bf16)
            if u < LANES - 1:
                pltpu.make_async_remote_copy(
                    src_ref=chunk1(send1, jc, u), dst_ref=landing1(jc, lane),
                    send_sem=send_sem1, recv_sem=recv_sem1.at[jc],
                    device_id={"fft": dest}, device_id_type=MESH,
                ).start()
            else:
                pltpu.make_async_copy(chunk1(send1, jc, u), landing1(jc, lane), own_sem1.at[jc]).start()
        return carry

    lax.fori_loop(0, NC, transform_b, 0)

    def response(j, carry):
        chirp_copy(j).wait()
        c, s = cos_sin(chirp_v[j])
        turn_v[0, j] = c
        turn_v[1, j] = s
        return carry

    lax.fori_loop(0, 16, response, 0)
    for copy in late:
        copy.wait()
    for part in range(2):
        cols = pl.ds(part * 128, 128)
        re, im = cmul(base_v[0, :, cols], base_v[1, :, cols], lane_v[0], lane_v[1])
        base_v[0, :, cols] = re
        base_v[1, :, cols] = im

    wait_total(scale1.at[pl.ds(0, LANES - 1)], scale_sems.at[0, 1])

    def middle(j):
        half_scale = (scale1[...] * 0.5)[:, 0:1, :]
        half_scale = jnp.concatenate([half_scale, half_scale], axis=2)
        z = decode(recv1[j].astype(f32), half_scale).reshape(256, 256)
        zh, zl = split(z)
        o = dot3(ah_v[j], al_v[j], zh, zl)
        re, im = cmul(o[:128], o[128:], turn_v[0, j], turn_v[1, j])
        ph, pll = split(jnp.concatenate([re, im], axis=0))
        o = dot3(bh_v[j], bl_v[j], ph, pll)
        re, im = cmul(o[:128], o[128:], base_v[0], base_v[1])
        power = jnp.sum((re * re + im * im).reshape(16, 8, 256), axis=0)
        return jnp.concatenate([re.T, im.T], axis=0), power

    def middle_chunk(jc, energy):
        wait_total(recv1.at[pl.ds(jc * JC, JC), pl.ds(0, LANES - 1)], recv_sem1.at[jc])
        wait_total(landing1(jc, lane), own_sem1.at[jc])
        parts = []
        for r in range(JC):
            part, power = middle(jc * JC + r)
            parts.append(part)
            energy = energy + power
        high, low = split(jnp.concatenate(parts, axis=1))
        u_v[:, aligned(jc, JC * 128)] = dot3(hh_v[...], hl_v[...], high, low)
        return energy

    energy = lax.fori_loop(0, NC, middle_chunk, jnp.zeros((8, 256), f32))
    my_scale = scale_of((energy[:, :128] + energy[:, 128:]) * (1.0 / 128.0))
    send_scale(my_scale, scale2_out, scale2, scale_sems.at[1])
    inverse2 = (1.0 / my_scale)[0:1, :]

    def post(q, carry):
        def rows_of(rt, inner):
            top = aligned(rt, 8)
            high = pl.ds(pl.multiple_of(q * 4 * RQ + rt * 8, 8), 8)
            low = pl.ds(pl.multiple_of(q * 4 * RQ + 2 * RQ + rt * 8, 8), 8)
            table = pl.ds(pl.multiple_of(q * 2 * RQ + rt * 8, 8), 8)
            tr, ti = cj_v[0, table, :], cj_v[1, table, :]
            x = []
            for j in range(16):
                cols = pl.ds(j * 128, 128)
                x.append(cmul(u_v[high, cols], u_v[low, cols], tr[:, j : j + 1], ti[:, j : j + 1]))
            x = radix16(x, 1)
            for l in range(16):
                re, im = cmul(*x[l], s2_ref[0, lane * 16 + l], s2_ref[1, lane * 16 + l])
                v_v[l, 0, top, :] = re
                v_v[l, 1, top, :] = im
            return inner

        lax.fori_loop(0, 2 * RQ // 8, rows_of, 0)

        for s in range(LANES):
            dest = peer(s)
            send2[dest, q] = encode(v_v[dest], inverse2[None]).astype(bf16)
            if s < LANES - 1:
                pltpu.make_async_remote_copy(
                    src_ref=send2.at[dest, q], dst_ref=recv2.at[q, lane],
                    send_sem=send_sem2, recv_sem=recv_sem2.at[q],
                    device_id={"fft": dest}, device_id_type=MESH,
                ).start()
            else:
                pltpu.make_async_copy(send2.at[dest, q], recv2.at[q, lane], own_sem2.at[q]).start()
        return carry

    lax.fori_loop(0, QC, post, 0)

    wait_total(scale2.at[pl.ds(0, LANES - 1)], scale_sems.at[1, 1])

    def out_copy(q):
        return pltpu.make_async_copy(stage.at[lax.rem(q, 2)], out_hbm.at[:, pl.ds(q * RQ, RQ), :], out_sem.at[q])

    def final(q, carry):
        wait_total(recv2.at[q, pl.ds(0, LANES - 1)], recv_sem2.at[q])
        wait_total(recv2.at[q, lane], own_sem2.at[q])

        def undo(source, inner):
            half_scale = (scale2[source] * 0.5)[0:1, :]
            z_v[source] = decode(recv2[q, source].astype(f32), half_scale[None])
            return inner

        lax.fori_loop(0, LANES, undo, 0)

        def rows_of(rt, inner):
            top = aligned(rt, 8)
            par, jt = rt // (RQ // 8), lax.rem(rt, RQ // 8)
            x = radix16([(z_v[s, 0, top, :], z_v[s, 1, top, :]) for s in range(16)], 1)
            for t in range(15):
                where = pl.ds(pl.multiple_of(t * RQ + jt * 8, 8), 8)
                xl_v[where, aligned(par, 128)] = x[t][0]
                xl_v[where, aligned(par + 2, 128)] = x[t][1]
            return inner

        lax.fori_loop(0, 2 * RQ // 8, rows_of, 0)

        @pl.when(q >= 2)
        def _():
            out_copy(q - 2).wait()

        def channels(block, inner):
            high, low = split(xl_v[aligned(block, 5 * RQ), :])
            y = dot3(high, low, qh_v[...], ql_v[...])
            re, im = y[:, :256], y[:, 256:]
            stage[lax.rem(q, 2), pl.ds(block * 5, 5)] = (re * re + im * im).reshape(5, RQ, 256)
            return inner

        lax.fori_loop(0, 3, channels, 0)
        out_copy(q).start()
        return carry

    lax.fori_loop(0, QC, final, 0)
    out_copy(QC - 2).wait()
    out_copy(QC - 1).wait()

    @pl.when(seg > 0)
    def _():
        head.wait_send()

    wait_total(scale1.at[pl.ds(0, LANES - 1)], scale_sems.at[0, 0])
    wait_total(scale2.at[pl.ds(0, LANES - 1)], scale_sems.at[1, 0])
    wait_total(send1.at[pl.ds(0, LANES - 1)], send_sem1)
    wait_total(send2.at[pl.ds(0, LANES - 1)], send_sem2)


def on_device(baseband, chirp_phase):
    own = baseband.reshape(16, OWN)
    t = tables()
    constants = [
        t["s1"], t["s2"], t["pw"], *t["g"], t["c2"], *t["a"], *t["b"], t["base"], t["gl"], *t["h"], t["cj"], *t["q"],
    ]
    constants = [jnp.asarray(c) for c in constants]
    anywhere = pl.BlockSpec(memory_space=pl.ANY)
    scalars = pl.BlockSpec(memory_space=pltpu.SMEM)
    v = lambda shape, kind=f32: pltpu.VMEM(shape, kind)
    dma = pltpu.SemaphoreType.DMA
    out = pl.pallas_call(
        kernel,
        out_shape=jax.ShapeDtypeStruct((15, 128, 256), f32),
        in_specs=[anywhere, anywhere, scalars, scalars] + [anywhere] * (len(constants) - 2),
        out_specs=anywhere,
        scratch_shapes=[
            v((16, COLS), bf16), v((2, 16, 16, 8, 256)), v((2, 16, 16, 8, 256)),
            v((JC * 128, 512), bf16), v((JC * 128, 512), bf16), v((JC * 128, 512)),
            v((16, 16, 16, 256), bf16), v((16, 16, 16, 256), bf16),
            v((16, QC, 2, 2 * RQ, 128), bf16), v((QC, 16, 2, 2 * RQ, 128), bf16),
            v((8, 128)), v((16, 8, 128)), v((8, 128)), v((16, 8, 128)),
            v((512, 512), bf16), v((512, 512), bf16), v((2, 8, 256)),
            v((16, 256, 256), bf16), v((16, 256, 256), bf16), v((16, 256, 256), bf16), v((16, 256, 256), bf16),
            v((2, 128, 256)), v((2, 128, 128)),
            v((512, 512), bf16), v((512, 512), bf16), v((2, 256, 128)),
            v((512, 512), bf16), v((512, 512), bf16),
            v((16, 128, 256)), v((2, 16, 128, 256)),
            v((512, 2048)),
            v((16, 2, 2 * RQ, 128)), v((16, 2, 2 * RQ, 128)), v((15 * RQ, 512)), v((2, 15, RQ, 256)),
            dma((16,)), dma((16,)), dma((2,)), dma((2, 2)), dma, dma((NC,)), dma((NC,)), dma, dma((QC,)),
            dma((QC,)), dma((QC,)),
        ],
        compiler_params=pltpu.CompilerParams(
            collective_id=0, has_side_effects=True, vmem_limit_bytes=60 * 1024 * 1024
        ),
        name="dedisperse",
    )(own, chirp_phase.reshape(128, 16, 256), *constants)
    return out.reshape(1, 15, 1, 128, 256)


def solution(mesh):
    return jax.shard_map(
        on_device,
        mesh=mesh,
        in_specs=(P("seg", "fft", None, None, None, None), P("fft", None, None, None)),
        out_specs=P("seg", None, "fft", None, None),
        check_vma=False,
    )
```

```python
import functools

import jax
import jax.numpy as jnp
import ml_dtypes
import numpy as np
from jax import lax
from jax.experimental import pallas as pl
from jax.experimental.pallas import tpu as pltpu
from jax.sharding import PartitionSpec as P

FFT_LEN = 8388608
LANES = 16
SEGS = 16
OWN = 61440
TAIL = 4096
COLS = OWN + TAIL
JC = 2
NC = 16 // JC
QC = 8
RQ = 16
KNEE = 4.0
POWER = 20
SHIFT = 2.0**-6.25
TINY = 1e-36

MESH = pl.DeviceIdType.MESH
f32 = jnp.float32
bf16 = jnp.bfloat16


def unit(numerator, modulus, direction):
    angle = (np.asarray(numerator, np.int64) % modulus) * (direction * 2.0 * np.pi / modulus)
    return np.cos(angle), np.sin(angle)


def halves(table):
    table = table.astype(np.float32)
    high = table.astype(ml_dtypes.bfloat16)
    low = (table - high.astype(np.float32)).astype(ml_dtypes.bfloat16)
    return high, low


@functools.lru_cache(maxsize=None)
def tables():
    n = FFT_LEN
    r16, r128, r256 = np.arange(16), np.arange(128), np.arange(256)
    out = {}
    c, s = unit(
        r16[None, :, None] * r16[None, None, :] * (n // 256) + r16[:, None, None] * r16[None, None, :],
        n,
        -1,
    )
    out["s1"] = np.stack([c, s]).astype(np.float32).reshape(2, -1)
    c, s = unit(r16[:, None] * r16[None, :], 256, 1)
    out["s2"] = np.stack([c, s])
    scalars = np.zeros((16, 2, 640), np.float32)
    scalars[:, :, :256] = out["s1"].reshape(2, 16, 256).transpose(1, 0, 2)
    scalars[:, :, 512:528] = out["s2"].transpose(1, 0, 2)
    out["scalars"] = scalars
    e = r16[:, None] + 16 * r16[None, :]
    ib = 16 * np.arange(8)[:, None] + 128 * r256[None, :]
    c, s = unit(e[:, :, None, None] * ib[None, None], n, -1)
    out["pw"] = np.stack([c, s]).astype(np.float32)
    c, s = unit(r256[:, None] * r256[None, :], 256, -1)
    out["g"] = halves(np.block([[c, s], [-s, c]]))
    res = r16[:, None] + 16 * np.arange(8)[None, :]
    c, s = unit(res[:, :, None] * r256[None, None, :], 32768, -1)
    out["c2"] = np.stack([c, s], axis=1).astype(np.float32)
    src, i = r16[:, None], np.arange(8)[None, :]
    num = (src + 16 * i)[None, None] * r128[None, :, None, None] * (n // 128)
    num = num + src[None, None] * 16 * r16[:, None, None, None]
    c, s = unit(num, n, -1)
    full = np.zeros((16, 2, 128, 16, 2, 8))
    full[:, 0, :, :, 0], full[:, 0, :, :, 1] = c, -s
    full[:, 1, :, :, 0], full[:, 1, :, :, 1] = s, c
    out["a"] = halves(full.reshape(16, 256, 256))
    num = r128[None, :, None] * r128[None, None, :] * (n // 128) + r128[None, :, None] * 16 * r16[:, None, None]
    c, s = unit(num, n, 1)
    out["b"] = halves(np.concatenate([np.concatenate([c, -s], 2), np.concatenate([s, c], 2)], 1))
    c, s = unit(r128[:, None] * r256[None, :], 32768, 1)
    out["base"] = np.stack([c, s]).astype(np.float32)
    c, s = unit(r16[:, None] * r128[None, :], n, 1)
    gl = np.stack([c, s], axis=1).astype(np.float32)
    out["gl"] = np.ascontiguousarray(np.broadcast_to(gl[..., None], gl.shape + (128,)))
    q, par, jj = np.meshgrid(np.arange(QC), np.arange(2), np.arange(RQ), indexing="ij")
    hh = 2 * (RQ * q + jj) + par
    hh = hh.reshape(QC, 2 * RQ)
    c, s = unit(hh[:, :, None] * r256[None, None, :], 256, 1)
    both = np.concatenate([np.concatenate([c, -s], 2), np.concatenate([s, c], 2)], 1)
    out["h"] = halves(both.reshape(512, 512))
    e = r16[:, None] + 16 * r16[None, :]
    c, s = unit(hh.reshape(1, 256, 1) * e[:, None, :], 65536, 1)
    cj = np.zeros((16, 2, 256, 128), np.float32)
    cj[:, 0, :, :16], cj[:, 1, :, :16] = c, s
    out["cj"] = cj
    r = np.arange(256)
    c, s = unit(r[:, None] * r256[None, :], 256, -1)
    out["q"] = halves(np.block([[c, s], [-s, c]]) * 2.0**-27)
    return out


def cmul(ar, ai, br, bi):
    return ar * br - ai * bi, ar * bi + ai * br


def radix4(x, sign):
    (ar, ai), (br, bi), (cr, ci), (dr, di) = x
    pr, pi, mr, mi = ar + cr, ai + ci, ar - cr, ai - ci
    qr, qi, nr, ni = br + dr, bi + di, br - dr, bi - di
    if sign > 0:
        ur, ui = -ni, nr
        return [(pr + qr, pi + qi), (mr - ni, mi + nr), (pr - qr, pi - qi), (mr + ni, mi - nr)]
    return [(pr + qr, pi + qi), (mr + ni, mi - nr), (pr - qr, pi - qi), (mr - ni, mi + nr)]


def turn(x, power, sign):
    xr, xi = x
    power = power % 16
    if power == 0:
        return x
    if power == 4:
        return (-xi, xr) if sign > 0 else (xi, -xr)
    root = float(np.sqrt(0.5))
    if power == 2:
        return ((xr - xi) * root, (xr + xi) * root) if sign > 0 else ((xr + xi) * root, (xi - xr) * root)
    if power == 6:
        return ((-xr - xi) * root, (xr - xi) * root) if sign > 0 else ((xi - xr) * root, (-xr - xi) * root)
    c = float(np.cos(2 * np.pi * power / 16))
    s = float(sign * np.sin(2 * np.pi * power / 16))
    return (xr * c - xi * s, xr * s + xi * c)


def radix16(x, sign):
    inner = [radix4([x[4 * n1 + n2] for n1 in range(4)], sign) for n2 in range(4)]
    out = [None] * 16
    for k1 in range(4):
        column = radix4([turn(inner[n2][k1], n2 * k1, sign) for n2 in range(4)], sign)
        for k2 in range(4):
            out[k1 + 4 * k2] = column[k2]
    return out


def split(x):
    high = x.astype(bf16)
    return high, (x - high.astype(f32)).astype(bf16)


def dot(a, b):
    return lax.dot_general(a, b, (((1,), (0,)), ((), ())), preferred_element_type=f32)


def dot3(ah, al, bh, bl):
    return dot(ah, bh) + dot(al, bh) + dot(ah, bl)


def encode(x, inverse):
    a = jnp.abs(x) * inverse
    v = a * a + 1.0
    w = (a + v * lax.rsqrt(v)) * SHIFT
    w2 = w * w
    w4 = w2 * w2
    w8 = w4 * w4
    y = (w8 * w8) * w4
    return jnp.where(x < 0, -y, y)


def decode(y, half_scale):
    t = jnp.log(jnp.abs(y)) * (1.0 / POWER) + float(-np.log(SHIFT))
    w = jnp.exp(t)
    a = (w - jnp.exp(-t)) * half_scale
    return jnp.where(y < 0, -a, a)


def cos_sin(x):
    y = x * 0.5
    z = y * y
    s = 1.0 / 6227020800.0
    for factor in (-1.0 / 39916800.0, 1.0 / 362880.0, -1.0 / 5040.0, 1.0 / 120.0, -1.0 / 6.0, 1.0):
        s = s * z + factor
    s = s * y
    c = 1.0 / 479001600.0
    for factor in (-1.0 / 3628800.0, 1.0 / 40320.0, -1.0 / 720.0, 1.0 / 24.0, -0.5, 1.0):
        c = c * z + factor
    return 1.0 - 2.0 * s * s, 2.0 * s * c


def aligned(index, size):
    return pl.ds(pl.multiple_of(index * size, size), size)


def kernel(
    x_hbm, chirp_hbm, scalars_hbm, pw_hbm, gh_hbm, gl_hbm, c2_hbm, ah_hbm, al_hbm, bh_hbm, bl_hbm,
    base_hbm, lane_hbm, hh_hbm, hl_hbm, cj_hbm, qh_hbm, ql_hbm,
    out_hbm,
    scalars, x_v, d_v, pw_v, lhs_h, lhs_l, y_v, send1, recv1, send2, recv2, scale1_out, scale1, scale2_out, scale2,
    gh_v, gl_v, c2_v, ah_v, al_v, bh_v, bl_v, base_v, lane_v, hh_v, hl_v, cj_v, qh_v, ql_v,
    chirp_v, turn_v, u_v, v_v, z_v, xl_v, stage,
    load_sem, chirp_sem, head_sems, scale_sems, send_sem1, recv_sem1, own_sem1, send_sem2, recv_sem2, own_sem2,
    out_sem,
):
    lane = lax.axis_index("fft")
    seg = lax.axis_index("seg")
    lane_x, lane_z = lane // 4, lax.rem(lane, 4)

    def peer(turn_index):
        step_z, step_x = (2, 1, 3, 0)[turn_index // 4], (turn_index + 1) % 4
        return lax.rem(lane_x + step_x, 4) * 4 + lax.rem(lane_z + step_z, 4)

    before, after = lax.rem(seg + SEGS - 1, SEGS), lax.rem(seg + 1, SEGS)

    def load(source, target, index):
        copy = pltpu.make_async_copy(source, target, load_sem.at[index])
        copy.start()
        return copy

    load_x = load(x_hbm, x_v.at[:, pl.ds(0, OWN)], 0)

    barrier = pltpu.get_barrier_semaphore()

    @pl.when(seg < SEGS - 1)
    def _():
        pl.semaphore_signal(barrier, inc=1, device_id={"seg": after}, device_id_type=MESH)

    for s in range(LANES - 1):
        pl.semaphore_signal(barrier, inc=1, device_id={"fft": peer(s)}, device_id_type=MESH)
    load_scalars = load(scalars_hbm.at[lane], scalars, 16)
    load_pw = load(pw_hbm, pw_v, 1)
    load_g = [load(gh_hbm, gh_v, 2), load(gl_hbm, gl_v, 3), load(c2_hbm.at[lane], c2_v, 4)]
    head = pltpu.make_async_remote_copy(
        src_ref=x_hbm.at[:, pl.ds(0, TAIL)], dst_ref=x_v.at[:, pl.ds(OWN, TAIL)],
        send_sem=head_sems.at[0], recv_sem=head_sems.at[1],
        device_id={"seg": before}, device_id_type=MESH,
    )

    @pl.when(seg > 0)
    def _():
        pl.semaphore_wait(barrier, LANES)
        head.start()

    @pl.when(seg == 0)
    def _():
        pl.semaphore_wait(barrier, LANES - 1)

    load_x.wait()
    load_scalars.wait()

    @pl.when(seg < SEGS - 1)
    def _():
        head.wait_recv()

    @pl.when(seg == SEGS - 1)
    def _():
        x_v[:, pl.ds(OWN, TAIL)] = jnp.zeros((16, TAIL), bf16)

    late = [
        load(ah_hbm, ah_v, 5), load(al_hbm, al_v, 6), load(bh_hbm, bh_v, 7), load(bl_hbm, bl_v, 8),
        load(base_hbm, base_v, 9), load(lane_hbm.at[lane], lane_v, 10), load(hh_hbm, hh_v, 11),
        load(hl_hbm, hl_v, 12), load(cj_hbm.at[lane], cj_v, 13), load(qh_hbm, qh_v, 14), load(ql_hbm, ql_v, 15),
    ]

    def chirp_copy(j):
        return pltpu.make_async_copy(chirp_hbm.at[:, j, :], chirp_v.at[j], chirp_sem.at[j])

    def chirp_start(j, carry):
        chirp_copy(j).start()
        return carry

    lax.fori_loop(0, 16, chirp_start, 0)

    def first_pass(t, energy):
        a_lo, half = t // 2, lax.rem(t, 2)
        x = []
        for a_hi in range(16):
            block = x_v[:, aligned((16 * a_hi + a_lo) * 2 + half, 128)].astype(f32)
            re, im = block[:8], block[8:]
            energy = energy + (re * re + im * im)
            x.append((re, im))
        x = radix16(x, -1)
        for e_lo in range(16):
            where = a_lo * 16 + e_lo
            re, im = cmul(*x[e_lo], scalars[0, where], scalars[1, where])
            d_v[0, e_lo, a_lo, :, aligned(half, 128)] = re
            d_v[1, e_lo, a_lo, :, aligned(half, 128)] = im
        return energy

    energy = lax.fori_loop(0, 32, first_pass, jnp.zeros((8, 128), f32))

    def scale_of(energy):
        total = jnp.sum(jnp.sum(energy, axis=1, keepdims=True), axis=0, keepdims=True)
        mean = jnp.maximum(jnp.broadcast_to(total, (8, 128)), TINY)
        return mean * lax.rsqrt(mean) * (1.0 / KNEE)

    def send_scale(value, out_ref, in_ref, sems):
        out_ref[...] = value
        in_ref[lane] = value

        for s in range(LANES - 1):
            pltpu.make_async_remote_copy(
                src_ref=out_ref, dst_ref=in_ref.at[lane], send_sem=sems.at[0], recv_sem=sems.at[1],
                device_id={"fft": peer(s)}, device_id_type=MESH,
            ).start()

    def wait_total(ref, sem):
        pltpu.make_async_copy(ref, ref, sem).wait()

    my_scale = scale_of(energy * 0.125)
    inverse = 1.0 / my_scale
    inverse = jnp.concatenate([inverse, inverse], axis=1)

    load_pw.wait()

    def second_pass(t, carry):
        e_lo, half = t // 2, lax.rem(t, 2)
        cols = aligned(half, 128)
        x = [(d_v[0, e_lo, a_lo, :, cols], d_v[1, e_lo, a_lo, :, cols]) for a_lo in range(16)]
        x = radix16(x, -1)
        for e_hi in range(16):
            re, im = cmul(*x[e_hi], pw_v[0, e_lo, e_hi, :, cols], pw_v[1, e_lo, e_hi, :, cols])
            d_v[0, e_lo, e_hi, :, cols] = re
            d_v[1, e_lo, e_hi, :, cols] = im
        return carry

    lax.fori_loop(0, 32, second_pass, 0)

    for copy in load_g:
        copy.wait()
    send_scale(my_scale, scale1_out, scale1, scale_sems.at[0])

    def chunk1(ref, jc, s):
        return ref.at[peer(s), pl.ds(jc * JC, JC)]

    def landing1(jc, source):
        return recv1.at[pl.ds(jc * JC, JC), source]

    rows = JC * 8

    def transform_b(jc, carry):
        for u in range(LANES):
            dest = peer(u)
            re = d_v[0, dest, pl.ds(jc * JC, JC)].reshape(rows, 256)
            im = d_v[1, dest, pl.ds(jc * JC, JC)].reshape(rows, 256)
            high, low = split(jnp.concatenate([re, im], axis=1))
            lhs_h[pl.ds(u * rows, rows), :] = high
            lhs_l[pl.ds(u * rows, rows), :] = low
        y_v[...] = dot3(lhs_h[...], lhs_l[...], gh_v[...], gl_v[...])
        cr, ci = c2_v[0][None], c2_v[1][None]
        for u in range(LANES):
            dest = peer(u)
            block = y_v[pl.ds(u * rows, rows), :]
            re = block[:, :256].reshape(JC, 8, 256)
            im = block[:, 256:].reshape(JC, 8, 256)
            re, im = cmul(re, im, cr, ci)
            coded = jnp.concatenate([encode(re, inverse[None]), encode(im, inverse[None])], axis=1)
            send1[dest, pl.ds(jc * JC, JC)] = coded.astype(bf16)
            if u < LANES - 1:
                pltpu.make_async_remote_copy(
                    src_ref=chunk1(send1, jc, u), dst_ref=landing1(jc, lane),
                    send_sem=send_sem1, recv_sem=recv_sem1.at[jc],
                    device_id={"fft": dest}, device_id_type=MESH,
                ).start()
            else:
                pltpu.make_async_copy(chunk1(send1, jc, u), landing1(jc, lane), own_sem1.at[jc]).start()
        return carry

    lax.fori_loop(0, NC, transform_b, 0)

    def response(j, carry):
        chirp_copy(j).wait()
        c, s = cos_sin(chirp_v[j])
        turn_v[0, j] = c
        turn_v[1, j] = s
        return carry

    lax.fori_loop(0, 16, response, 0)
    for copy in late:
        copy.wait()
    for part in range(2):
        cols = pl.ds(part * 128, 128)
        re, im = cmul(base_v[0, :, cols], base_v[1, :, cols], lane_v[0], lane_v[1])
        base_v[0, :, cols] = re
        base_v[1, :, cols] = im

    wait_total(scale1.at[pl.ds(0, LANES - 1)], scale_sems.at[0, 1])

    def middle(j):
        half_scale = (scale1[...] * 0.5)[:, 0:1, :]
        half_scale = jnp.concatenate([half_scale, half_scale], axis=2)
        z = decode(recv1[j].astype(f32), half_scale).reshape(256, 256)
        zh, zl = split(z)
        o = dot3(ah_v[j], al_v[j], zh, zl)
        re, im = cmul(o[:128], o[128:], turn_v[0, j], turn_v[1, j])
        ph, pll = split(jnp.concatenate([re, im], axis=0))
        o = dot3(bh_v[j], bl_v[j], ph, pll)
        re, im = cmul(o[:128], o[128:], base_v[0], base_v[1])
        power = jnp.sum((re * re + im * im).reshape(16, 8, 256), axis=0)
        return jnp.concatenate([re.T, im.T], axis=0), power

    def middle_chunk(jc, energy):
        wait_total(recv1.at[pl.ds(jc * JC, JC), pl.ds(0, LANES - 1)], recv_sem1.at[jc])
        wait_total(landing1(jc, lane), own_sem1.at[jc])
        parts = []
        for r in range(JC):
            part, power = middle(jc * JC + r)
            parts.append(part)
            energy = energy + power
        high, low = split(jnp.concatenate(parts, axis=1))
        u_v[:, aligned(jc, JC * 128)] = dot3(hh_v[...], hl_v[...], high, low)
        return energy

    energy = lax.fori_loop(0, NC, middle_chunk, jnp.zeros((8, 256), f32))
    my_scale = scale_of((energy[:, :128] + energy[:, 128:]) * (1.0 / 128.0))
    send_scale(my_scale, scale2_out, scale2, scale_sems.at[1])
    inverse2 = (1.0 / my_scale)[0:1, :]

    def post(q, carry):
        def rows_of(rt, inner):
            top = aligned(rt, 8)
            high = pl.ds(pl.multiple_of(q * 4 * RQ + rt * 8, 8), 8)
            low = pl.ds(pl.multiple_of(q * 4 * RQ + 2 * RQ + rt * 8, 8), 8)
            table = pl.ds(pl.multiple_of(q * 2 * RQ + rt * 8, 8), 8)
            tr, ti = cj_v[0, table, :], cj_v[1, table, :]
            x = []
            for j in range(16):
                cols = pl.ds(j * 128, 128)
                x.append(cmul(u_v[high, cols], u_v[low, cols], tr[:, j : j + 1], ti[:, j : j + 1]))
            x = radix16(x, 1)
            for l in range(16):
                re, im = cmul(*x[l], scalars[0, 512 + l], scalars[1, 512 + l])
                v_v[l, 0, top, :] = re
                v_v[l, 1, top, :] = im
            return inner

        lax.fori_loop(0, 2 * RQ // 8, rows_of, 0)

        for s in range(LANES):
            dest = peer(s)
            send2[dest, q] = encode(v_v[dest], inverse2[None]).astype(bf16)
            if s < LANES - 1:
                pltpu.make_async_remote_copy(
                    src_ref=send2.at[dest, q], dst_ref=recv2.at[q, lane],
                    send_sem=send_sem2, recv_sem=recv_sem2.at[q],
                    device_id={"fft": dest}, device_id_type=MESH,
                ).start()
            else:
                pltpu.make_async_copy(send2.at[dest, q], recv2.at[q, lane], own_sem2.at[q]).start()
        return carry

    lax.fori_loop(0, QC, post, 0)

    wait_total(scale2.at[pl.ds(0, LANES - 1)], scale_sems.at[1, 1])

    def out_copy(q):
        return pltpu.make_async_copy(stage.at[lax.rem(q, 2)], out_hbm.at[:, pl.ds(q * RQ, RQ), :], out_sem.at[q])

    def final(q, carry):
        wait_total(recv2.at[q, pl.ds(0, LANES - 1)], recv_sem2.at[q])
        wait_total(recv2.at[q, lane], own_sem2.at[q])

        def undo(source, inner):
            half_scale = (scale2[source] * 0.5)[0:1, :]
            z_v[source] = decode(recv2[q, source].astype(f32), half_scale[None])
            return inner

        lax.fori_loop(0, LANES, undo, 0)

        def rows_of(rt, inner):
            top = aligned(rt, 8)
            par, jt = rt // (RQ // 8), lax.rem(rt, RQ // 8)
            x = radix16([(z_v[s, 0, top, :], z_v[s, 1, top, :]) for s in range(16)], 1)
            for t in range(15):
                where = pl.ds(pl.multiple_of(t * RQ + jt * 8, 8), 8)
                xl_v[where, aligned(par, 128)] = x[t][0]
                xl_v[where, aligned(par + 2, 128)] = x[t][1]
            return inner

        lax.fori_loop(0, 2 * RQ // 8, rows_of, 0)

        @pl.when(q >= 2)
        def _():
            out_copy(q - 2).wait()

        high, low = split(xl_v[...])
        y = dot3(high, low, qh_v[...], ql_v[...])
        re, im = y[:, :256], y[:, 256:]
        stage[lax.rem(q, 2)] = (re * re + im * im).reshape(15, RQ, 256)
        out_copy(q).start()
        return carry

    lax.fori_loop(0, QC, final, 0)
    out_copy(QC - 2).wait()
    out_copy(QC - 1).wait()

    @pl.when(seg > 0)
    def _():
        head.wait_send()

    wait_total(scale1.at[pl.ds(0, LANES - 1)], scale_sems.at[0, 0])
    wait_total(scale2.at[pl.ds(0, LANES - 1)], scale_sems.at[1, 0])
    wait_total(send1.at[pl.ds(0, LANES - 1)], send_sem1)
    wait_total(send2.at[pl.ds(0, LANES - 1)], send_sem2)


def on_device(baseband, chirp_phase):
    own = baseband.reshape(16, OWN)
    t = tables()
    constants = [
        t["scalars"], t["pw"], *t["g"], t["c2"], *t["a"], *t["b"], t["base"], t["gl"], *t["h"], t["cj"], *t["q"],
    ]
    constants = [jnp.asarray(c) for c in constants]
    anywhere = pl.BlockSpec(memory_space=pl.ANY)
    v = lambda shape, kind=f32: pltpu.VMEM(shape, kind)
    dma = pltpu.SemaphoreType.DMA
    out = pl.pallas_call(
        kernel,
        out_shape=jax.ShapeDtypeStruct((15, 128, 256), f32),
        in_specs=[anywhere] * (len(constants) + 2),
        out_specs=anywhere,
        scratch_shapes=[
            pltpu.SMEM((2, 640), f32), v((16, COLS), bf16), v((2, 16, 16, 8, 256)), v((2, 16, 16, 8, 256)),
            v((JC * 128, 512), bf16), v((JC * 128, 512), bf16), v((JC * 128, 512)),
            v((16, 16, 16, 256), bf16), v((16, 16, 16, 256), bf16),
            v((16, QC, 2, 2 * RQ, 128), bf16), v((QC, 16, 2, 2 * RQ, 128), bf16),
            v((8, 128)), v((16, 8, 128)), v((8, 128)), v((16, 8, 128)),
            v((512, 512), bf16), v((512, 512), bf16), v((2, 8, 256)),
            v((16, 256, 256), bf16), v((16, 256, 256), bf16), v((16, 256, 256), bf16), v((16, 256, 256), bf16),
            v((2, 128, 256)), v((2, 128, 128)),
            v((512, 512), bf16), v((512, 512), bf16), v((2, 256, 128)),
            v((512, 512), bf16), v((512, 512), bf16),
            v((16, 128, 256)), v((2, 16, 128, 256)),
            v((512, 2048)),
            v((16, 2, 2 * RQ, 128)), v((16, 2, 2 * RQ, 128)), v((15 * RQ, 512)), v((2, 15, RQ, 256)),
            dma((17,)), dma((16,)), dma((2,)), dma((2, 2)), dma, dma((NC,)), dma((NC,)), dma, dma((QC,)),
            dma((QC,)), dma((QC,)),
        ],
        compiler_params=pltpu.CompilerParams(
            collective_id=0, has_side_effects=True, vmem_limit_bytes=60 * 1024 * 1024
        ),
        name="dedisperse",
    )(own, chirp_phase.reshape(128, 16, 256), *constants)
    return out.reshape(1, 15, 1, 128, 256)


def solution(mesh):
    return jax.shard_map(
        on_device,
        mesh=mesh,
        in_specs=(P("seg", "fft", None, None, None, None), P("fft", None, None, None)),
        out_specs=P("seg", None, "fft", None, None),
        check_vma=False,
    )
```

```python
import functools

import jax
import jax.numpy as jnp
import ml_dtypes
import numpy as np
from jax import lax
from jax.experimental import pallas as pl
from jax.experimental.pallas import tpu as pltpu
from jax.sharding import PartitionSpec as P

FFT_LEN = 8388608
LANES = 16
SEGS = 16
OWN = 61440
TAIL = 4096
COLS = OWN + TAIL
JC = 2
NC = 16 // JC
QC = 8
RQ = 16
KNEE = 4.0
POWER = 20
SHIFT = 2.0**-6.25
TINY = 1e-36

MESH = pl.DeviceIdType.MESH
f32 = jnp.float32
bf16 = jnp.bfloat16


def unit(numerator, modulus, direction):
    angle = (np.asarray(numerator, np.int64) % modulus) * (direction * 2.0 * np.pi / modulus)
    return np.cos(angle), np.sin(angle)


def halves(table):
    table = table.astype(np.float32)
    high = table.astype(ml_dtypes.bfloat16)
    low = (table - high.astype(np.float32)).astype(ml_dtypes.bfloat16)
    return high, low


@functools.lru_cache(maxsize=None)
def tables():
    n = FFT_LEN
    r16, r128, r256 = np.arange(16), np.arange(128), np.arange(256)
    out = {}
    c, s = unit(
        r16[None, :, None] * r16[None, None, :] * (n // 256) + r16[:, None, None] * r16[None, None, :],
        n,
        -1,
    )
    out["s1"] = np.stack([c, s]).astype(np.float32).reshape(2, -1)
    c, s = unit(r16[:, None] * r16[None, :], 256, 1)
    out["s2"] = np.stack([c, s])
    scalars = np.zeros((16, 2, 640), np.float32)
    scalars[:, :, :256] = out["s1"].reshape(2, 16, 256).transpose(1, 0, 2)
    scalars[:, :, 512:528] = out["s2"].transpose(1, 0, 2)
    out["scalars"] = scalars
    e = r16[:, None] + 16 * r16[None, :]
    ib = 16 * np.arange(8)[:, None] + 128 * r256[None, :]
    c, s = unit(e[:, :, None, None] * ib[None, None], n, -1)
    out["pw"] = np.stack([c, s]).astype(np.float32)
    c, s = unit(r256[:, None] * r256[None, :], 256, -1)
    out["g"] = halves(np.block([[c, s], [-s, c]]))
    res = r16[:, None] + 16 * np.arange(8)[None, :]
    c, s = unit(res[:, :, None] * r256[None, None, :], 32768, -1)
    out["c2"] = np.stack([c, s], axis=1).astype(np.float32)
    src, i = r16[:, None], np.arange(8)[None, :]
    num = (src + 16 * i)[None, None] * r128[None, :, None, None] * (n // 128)
    num = num + src[None, None] * 16 * r16[:, None, None, None]
    c, s = unit(num, n, -1)
    full = np.zeros((16, 2, 128, 16, 2, 8))
    full[:, 0, :, :, 0], full[:, 0, :, :, 1] = c, -s
    full[:, 1, :, :, 0], full[:, 1, :, :, 1] = s, c
    out["a"] = halves(full.reshape(16, 256, 256))
    num = r128[None, :, None] * r128[None, None, :] * (n // 128) + r128[None, :, None] * 16 * r16[:, None, None]
    c, s = unit(num, n, 1)
    out["b"] = halves(np.concatenate([np.concatenate([c, -s], 2), np.concatenate([s, c], 2)], 1))
    c, s = unit(r128[:, None] * r256[None, :], 32768, 1)
    out["base"] = np.stack([c, s]).astype(np.float32)
    c, s = unit(r16[:, None] * r128[None, :], n, 1)
    gl = np.stack([c, s], axis=1).astype(np.float32)
    out["gl"] = np.ascontiguousarray(np.broadcast_to(gl[..., None], gl.shape + (128,)))
    q, par, jj = np.meshgrid(np.arange(QC), np.arange(2), np.arange(RQ), indexing="ij")
    hh = 2 * (RQ * q + jj) + par
    hh = hh.reshape(QC, 2 * RQ)
    c, s = unit(hh[:, :, None] * r256[None, None, :], 256, 1)
    both = np.concatenate([np.concatenate([c, -s], 2), np.concatenate([s, c], 2)], 1)
    out["h"] = halves(both.reshape(512, 512))
    e = r16[:, None] + 16 * r16[None, :]
    c, s = unit(hh.reshape(1, 256, 1) * e[:, None, :], 65536, 1)
    cj = np.zeros((16, 2, 256, 128), np.float32)
    cj[:, 0, :, :16], cj[:, 1, :, :16] = c, s
    out["cj"] = cj
    r = np.arange(256)
    c, s = unit(r[:, None] * r256[None, :], 256, -1)
    out["q"] = halves(np.block([[c, s], [-s, c]]) * 2.0**-27)
    return out


def cmul(ar, ai, br, bi):
    return ar * br - ai * bi, ar * bi + ai * br


def radix4(x, sign):
    (ar, ai), (br, bi), (cr, ci), (dr, di) = x
    pr, pi, mr, mi = ar + cr, ai + ci, ar - cr, ai - ci
    qr, qi, nr, ni = br + dr, bi + di, br - dr, bi - di
    if sign > 0:
        ur, ui = -ni, nr
        return [(pr + qr, pi + qi), (mr - ni, mi + nr), (pr - qr, pi - qi), (mr + ni, mi - nr)]
    return [(pr + qr, pi + qi), (mr + ni, mi - nr), (pr - qr, pi - qi), (mr - ni, mi + nr)]


def turn(x, power, sign):
    xr, xi = x
    power = power % 16
    if power == 0:
        return x
    if power == 4:
        return (-xi, xr) if sign > 0 else (xi, -xr)
    root = float(np.sqrt(0.5))
    if power == 2:
        return ((xr - xi) * root, (xr + xi) * root) if sign > 0 else ((xr + xi) * root, (xi - xr) * root)
    if power == 6:
        return ((-xr - xi) * root, (xr - xi) * root) if sign > 0 else ((xi - xr) * root, (-xr - xi) * root)
    c = float(np.cos(2 * np.pi * power / 16))
    s = float(sign * np.sin(2 * np.pi * power / 16))
    return (xr * c - xi * s, xr * s + xi * c)


def radix16(x, sign):
    inner = [radix4([x[4 * n1 + n2] for n1 in range(4)], sign) for n2 in range(4)]
    out = [None] * 16
    for k1 in range(4):
        column = radix4([turn(inner[n2][k1], n2 * k1, sign) for n2 in range(4)], sign)
        for k2 in range(4):
            out[k1 + 4 * k2] = column[k2]
    return out


def split(x):
    high = x.astype(bf16)
    return high, (x - high.astype(f32)).astype(bf16)


def dot(a, b):
    return lax.dot_general(a, b, (((1,), (0,)), ((), ())), preferred_element_type=f32)


def dot3(ah, al, bh, bl):
    return dot(ah, bh) + dot(al, bh) + dot(ah, bl)


def encode(x, inverse):
    a = jnp.abs(x) * inverse
    v = a * a + 1.0
    w = (a + v * lax.rsqrt(v)) * SHIFT
    w2 = w * w
    w4 = w2 * w2
    w8 = w4 * w4
    y = (w8 * w8) * w4
    return jnp.where(x < 0, -y, y)


def decode(y, half_scale):
    t = jnp.log(jnp.abs(y)) * (1.0 / POWER) + float(-np.log(SHIFT))
    w = jnp.exp(t)
    a = (w - jnp.exp(-t)) * half_scale
    return jnp.where(y < 0, -a, a)


def cos_sin(x):
    y = x * 0.5
    z = y * y
    s = 1.0 / 6227020800.0
    for factor in (-1.0 / 39916800.0, 1.0 / 362880.0, -1.0 / 5040.0, 1.0 / 120.0, -1.0 / 6.0, 1.0):
        s = s * z + factor
    s = s * y
    c = 1.0 / 479001600.0
    for factor in (-1.0 / 3628800.0, 1.0 / 40320.0, -1.0 / 720.0, 1.0 / 24.0, -0.5, 1.0):
        c = c * z + factor
    return 1.0 - 2.0 * s * s, 2.0 * s * c


def aligned(index, size):
    return pl.ds(pl.multiple_of(index * size, size), size)


def head_kernel(x_hbm, tail_hbm, sems):
    seg = lax.axis_index("seg")
    phase = lax.rem(seg, 4)
    before, after = lax.rem(seg + SEGS - 1, SEGS), lax.rem(seg + 1, SEGS)
    barrier = pltpu.get_barrier_semaphore()
    head = pltpu.make_async_remote_copy(
        src_ref=x_hbm.at[:, pl.ds(0, TAIL)], dst_ref=tail_hbm, send_sem=sems.at[0], recv_sem=sems.at[1],
        device_id={"seg": before}, device_id_type=MESH,
    )

    @pl.when(phase != 3)
    def _():
        pl.semaphore_signal(barrier, inc=1, device_id={"seg": after}, device_id_type=MESH)

    @pl.when(phase != 0)
    def _():
        pl.semaphore_wait(barrier, 1)
        head.start()

    @pl.when(phase != 3)
    def _():
        head.wait_recv()

    @pl.when(phase != 0)
    def _():
        head.wait_send()


def kernel(
    x_hbm, tail_hbm, chirp_hbm, scalars_hbm, pw_hbm, gh_hbm, gl_hbm, c2_hbm, ah_hbm, al_hbm, bh_hbm, bl_hbm,
    base_hbm, lane_hbm, hh_hbm, hl_hbm, cj_hbm, qh_hbm, ql_hbm,
    out_hbm,
    scalars, x_v, d_v, pw_v, lhs_h, lhs_l, y_v, send1, recv1, send2, recv2, scale1_out, scale1, scale2_out, scale2,
    gh_v, gl_v, c2_v, ah_v, al_v, bh_v, bl_v, base_v, lane_v, hh_v, hl_v, cj_v, qh_v, ql_v,
    chirp_v, turn_v, u_v, v_v, z_v, xl_v, stage,
    load_sem, chirp_sem, head_sems, scale_sems, send_sem1, recv_sem1, own_sem1, send_sem2, recv_sem2, own_sem2,
    out_sem,
):
    lane = lax.axis_index("fft")
    seg = lax.axis_index("seg")
    lane_x, lane_z = lane // 4, lax.rem(lane, 4)

    def peer(turn_index):
        step_z, step_x = (2, 1, 3, 0)[turn_index // 4], (turn_index + 1) % 4
        return lax.rem(lane_x + step_x, 4) * 4 + lax.rem(lane_z + step_z, 4)

    phase = lax.rem(seg, 4)
    before, after = lax.rem(seg + SEGS - 1, SEGS), lax.rem(seg + 1, SEGS)

    def load(source, target, index):
        copy = pltpu.make_async_copy(source, target, load_sem.at[index])
        copy.start()
        return copy

    load_x = load(x_hbm, x_v.at[:, pl.ds(0, OWN)], 0)

    barrier = pltpu.get_barrier_semaphore()

    @pl.when((phase == 3) & (seg < SEGS - 1))
    def _():
        pl.semaphore_signal(barrier, inc=1, device_id={"seg": after}, device_id_type=MESH)

    for s in range(LANES - 1):
        pl.semaphore_signal(barrier, inc=1, device_id={"fft": peer(s)}, device_id_type=MESH)
    load_tail = pltpu.make_async_copy(tail_hbm, x_v.at[:, pl.ds(OWN, TAIL)], load_sem.at[17])
    pl.when(phase != 3)(load_tail.start)
    load_scalars = load(scalars_hbm.at[lane], scalars, 16)
    load_pw = load(pw_hbm, pw_v, 1)
    load_g = [load(gh_hbm, gh_v, 2), load(gl_hbm, gl_v, 3), load(c2_hbm.at[lane], c2_v, 4)]
    head = pltpu.make_async_remote_copy(
        src_ref=x_hbm.at[:, pl.ds(0, TAIL)], dst_ref=x_v.at[:, pl.ds(OWN, TAIL)],
        send_sem=head_sems.at[0], recv_sem=head_sems.at[1],
        device_id={"seg": before}, device_id_type=MESH,
    )
    load_x.wait()
    load_scalars.wait()
    pl.when(phase != 3)(load_tail.wait)
    pl.when((phase == 3) & (seg < SEGS - 1))(head.wait_recv)

    @pl.when(seg == SEGS - 1)
    def _():
        x_v[:, pl.ds(OWN, TAIL)] = jnp.zeros((16, TAIL), bf16)

    late = [
        load(ah_hbm, ah_v, 5), load(al_hbm, al_v, 6), load(bh_hbm, bh_v, 7), load(bl_hbm, bl_v, 8),
        load(base_hbm, base_v, 9), load(lane_hbm.at[lane], lane_v, 10), load(hh_hbm, hh_v, 11),
        load(hl_hbm, hl_v, 12), load(cj_hbm.at[lane], cj_v, 13), load(qh_hbm, qh_v, 14), load(ql_hbm, ql_v, 15),
    ]

    def chirp_copy(j):
        return pltpu.make_async_copy(chirp_hbm.at[:, j, :], chirp_v.at[j], chirp_sem.at[j])

    def chirp_start(j, carry):
        chirp_copy(j).start()
        return carry

    lax.fori_loop(0, 16, chirp_start, 0)

    def first_pass(t, energy):
        a_lo, half = t // 2, lax.rem(t, 2)
        x = []
        for a_hi in range(16):
            block = x_v[:, aligned((16 * a_hi + a_lo) * 2 + half, 128)].astype(f32)
            re, im = block[:8], block[8:]
            energy = energy + (re * re + im * im)
            x.append((re, im))
        x = radix16(x, -1)
        for e_lo in range(16):
            where = a_lo * 16 + e_lo
            re, im = cmul(*x[e_lo], scalars[0, where], scalars[1, where])
            d_v[0, e_lo, a_lo, :, aligned(half, 128)] = re
            d_v[1, e_lo, a_lo, :, aligned(half, 128)] = im
        return energy

    energy = lax.fori_loop(0, 32, first_pass, jnp.zeros((8, 128), f32))

    def scale_of(energy):
        total = jnp.sum(jnp.sum(energy, axis=1, keepdims=True), axis=0, keepdims=True)
        mean = jnp.maximum(jnp.broadcast_to(total, (8, 128)), TINY)
        return mean * lax.rsqrt(mean) * (1.0 / KNEE)

    def send_scale(value, out_ref, in_ref, sems):
        out_ref[...] = value
        in_ref[lane] = value

        for s in range(LANES - 1):
            pltpu.make_async_remote_copy(
                src_ref=out_ref, dst_ref=in_ref.at[lane], send_sem=sems.at[0], recv_sem=sems.at[1],
                device_id={"fft": peer(s)}, device_id_type=MESH,
            ).start()

    def wait_total(ref, sem):
        pltpu.make_async_copy(ref, ref, sem).wait()

    my_scale = scale_of(energy * 0.125)
    inverse = 1.0 / my_scale
    inverse = jnp.concatenate([inverse, inverse], axis=1)

    load_pw.wait()

    def second_pass(t, carry):
        e_lo, half = t // 2, lax.rem(t, 2)
        cols = aligned(half, 128)
        x = [(d_v[0, e_lo, a_lo, :, cols], d_v[1, e_lo, a_lo, :, cols]) for a_lo in range(16)]
        x = radix16(x, -1)
        for e_hi in range(16):
            re, im = cmul(*x[e_hi], pw_v[0, e_lo, e_hi, :, cols], pw_v[1, e_lo, e_hi, :, cols])
            d_v[0, e_lo, e_hi, :, cols] = re
            d_v[1, e_lo, e_hi, :, cols] = im
        return carry

    lax.fori_loop(0, 32, second_pass, 0)

    for copy in load_g:
        copy.wait()

    @pl.when((phase == 0) & (seg > 0))
    def _():
        pl.semaphore_wait(barrier, LANES)
        head.start()

    @pl.when((phase != 0) | (seg == 0))
    def _():
        pl.semaphore_wait(barrier, LANES - 1)

    send_scale(my_scale, scale1_out, scale1, scale_sems.at[0])

    def chunk1(ref, jc, s):
        return ref.at[peer(s), pl.ds(jc * JC, JC)]

    def landing1(jc, source):
        return recv1.at[pl.ds(jc * JC, JC), source]

    rows = JC * 8

    def transform_b(jc, carry):
        for u in range(LANES):
            dest = peer(u)
            re = d_v[0, dest, pl.ds(jc * JC, JC)].reshape(rows, 256)
            im = d_v[1, dest, pl.ds(jc * JC, JC)].reshape(rows, 256)
            high, low = split(jnp.concatenate([re, im], axis=1))
            lhs_h[pl.ds(u * rows, rows), :] = high
            lhs_l[pl.ds(u * rows, rows), :] = low
        y_v[...] = dot3(lhs_h[...], lhs_l[...], gh_v[...], gl_v[...])
        cr, ci = c2_v[0][None], c2_v[1][None]
        for u in range(LANES):
            dest = peer(u)
            block = y_v[pl.ds(u * rows, rows), :]
            re = block[:, :256].reshape(JC, 8, 256)
            im = block[:, 256:].reshape(JC, 8, 256)
            re, im = cmul(re, im, cr, ci)
            coded = jnp.concatenate([encode(re, inverse[None]), encode(im, inverse[None])], axis=1)
            send1[dest, pl.ds(jc * JC, JC)] = coded.astype(bf16)
            if u < LANES - 1:
                pltpu.make_async_remote_copy(
                    src_ref=chunk1(send1, jc, u), dst_ref=landing1(jc, lane),
                    send_sem=send_sem1, recv_sem=recv_sem1.at[jc],
                    device_id={"fft": dest}, device_id_type=MESH,
                ).start()
            else:
                pltpu.make_async_copy(chunk1(send1, jc, u), landing1(jc, lane), own_sem1.at[jc]).start()
        return carry

    lax.fori_loop(0, NC, transform_b, 0)

    def response(j, carry):
        chirp_copy(j).wait()
        c, s = cos_sin(chirp_v[j])
        turn_v[0, j] = c
        turn_v[1, j] = s
        return carry

    lax.fori_loop(0, 16, response, 0)
    for copy in late:
        copy.wait()
    for part in range(2):
        cols = pl.ds(part * 128, 128)
        re, im = cmul(base_v[0, :, cols], base_v[1, :, cols], lane_v[0], lane_v[1])
        base_v[0, :, cols] = re
        base_v[1, :, cols] = im

    wait_total(scale1.at[pl.ds(0, LANES - 1)], scale_sems.at[0, 1])

    def middle(j):
        half_scale = (scale1[...] * 0.5)[:, 0:1, :]
        half_scale = jnp.concatenate([half_scale, half_scale], axis=2)
        z = decode(recv1[j].astype(f32), half_scale).reshape(256, 256)
        zh, zl = split(z)
        o = dot3(ah_v[j], al_v[j], zh, zl)
        re, im = cmul(o[:128], o[128:], turn_v[0, j], turn_v[1, j])
        ph, pll = split(jnp.concatenate([re, im], axis=0))
        o = dot3(bh_v[j], bl_v[j], ph, pll)
        re, im = cmul(o[:128], o[128:], base_v[0], base_v[1])
        power = jnp.sum((re * re + im * im).reshape(16, 8, 256), axis=0)
        return jnp.concatenate([re.T, im.T], axis=0), power

    def middle_chunk(jc, energy):
        wait_total(recv1.at[pl.ds(jc * JC, JC), pl.ds(0, LANES - 1)], recv_sem1.at[jc])
        wait_total(landing1(jc, lane), own_sem1.at[jc])
        parts = []
        for r in range(JC):
            part, power = middle(jc * JC + r)
            parts.append(part)
            energy = energy + power
        high, low = split(jnp.concatenate(parts, axis=1))
        u_v[:, aligned(jc, JC * 128)] = dot3(hh_v[...], hl_v[...], high, low)
        return energy

    energy = lax.fori_loop(0, NC, middle_chunk, jnp.zeros((8, 256), f32))
    my_scale = scale_of((energy[:, :128] + energy[:, 128:]) * (1.0 / 128.0))
    send_scale(my_scale, scale2_out, scale2, scale_sems.at[1])
    inverse2 = (1.0 / my_scale)[0:1, :]

    def post(q, carry):
        def rows_of(rt, inner):
            top = aligned(rt, 8)
            high = pl.ds(pl.multiple_of(q * 4 * RQ + rt * 8, 8), 8)
            low = pl.ds(pl.multiple_of(q * 4 * RQ + 2 * RQ + rt * 8, 8), 8)
            table = pl.ds(pl.multiple_of(q * 2 * RQ + rt * 8, 8), 8)
            tr, ti = cj_v[0, table, :], cj_v[1, table, :]
            x = []
            for j in range(16):
                cols = pl.ds(j * 128, 128)
                x.append(cmul(u_v[high, cols], u_v[low, cols], tr[:, j : j + 1], ti[:, j : j + 1]))
            x = radix16(x, 1)
            for l in range(16):
                re, im = cmul(*x[l], scalars[0, 512 + l], scalars[1, 512 + l])
                v_v[l, 0, top, :] = re
                v_v[l, 1, top, :] = im
            return inner

        lax.fori_loop(0, 2 * RQ // 8, rows_of, 0)

        for s in range(LANES):
            dest = peer(s)
            send2[dest, q] = encode(v_v[dest], inverse2[None]).astype(bf16)
            if s < LANES - 1:
                pltpu.make_async_remote_copy(
                    src_ref=send2.at[dest, q], dst_ref=recv2.at[q, lane],
                    send_sem=send_sem2, recv_sem=recv_sem2.at[q],
                    device_id={"fft": dest}, device_id_type=MESH,
                ).start()
            else:
                pltpu.make_async_copy(send2.at[dest, q], recv2.at[q, lane], own_sem2.at[q]).start()
        return carry

    lax.fori_loop(0, QC, post, 0)

    wait_total(scale2.at[pl.ds(0, LANES - 1)], scale_sems.at[1, 1])

    def out_copy(q):
        return pltpu.make_async_copy(stage.at[lax.rem(q, 2)], out_hbm.at[:, pl.ds(q * RQ, RQ), :], out_sem.at[q])

    def final(q, carry):
        wait_total(recv2.at[q, pl.ds(0, LANES - 1)], recv_sem2.at[q])
        wait_total(recv2.at[q, lane], own_sem2.at[q])

        def undo(source, inner):
            half_scale = (scale2[source] * 0.5)[0:1, :]
            z_v[source] = decode(recv2[q, source].astype(f32), half_scale[None])
            return inner

        lax.fori_loop(0, LANES, undo, 0)

        def rows_of(rt, inner):
            top = aligned(rt, 8)
            par, jt = rt // (RQ // 8), lax.rem(rt, RQ // 8)
            x = radix16([(z_v[s, 0, top, :], z_v[s, 1, top, :]) for s in range(16)], 1)
            for t in range(15):
                where = pl.ds(pl.multiple_of(t * RQ + jt * 8, 8), 8)
                xl_v[where, aligned(par, 128)] = x[t][0]
                xl_v[where, aligned(par + 2, 128)] = x[t][1]
            return inner

        lax.fori_loop(0, 2 * RQ // 8, rows_of, 0)

        @pl.when(q >= 2)
        def _():
            out_copy(q - 2).wait()

        high, low = split(xl_v[...])
        y = dot3(high, low, qh_v[...], ql_v[...])
        re, im = y[:, :256], y[:, 256:]
        stage[lax.rem(q, 2)] = (re * re + im * im).reshape(15, RQ, 256)
        out_copy(q).start()
        return carry

    lax.fori_loop(0, QC, final, 0)
    out_copy(QC - 2).wait()
    out_copy(QC - 1).wait()

    @pl.when((phase == 0) & (seg > 0))
    def _():
        head.wait_send()

    wait_total(scale1.at[pl.ds(0, LANES - 1)], scale_sems.at[0, 0])
    wait_total(scale2.at[pl.ds(0, LANES - 1)], scale_sems.at[1, 0])
    wait_total(send1.at[pl.ds(0, LANES - 1)], send_sem1)
    wait_total(send2.at[pl.ds(0, LANES - 1)], send_sem2)


def on_device(baseband, chirp_phase):
    own = baseband.reshape(16, OWN)
    tail = pl.pallas_call(
        head_kernel,
        out_shape=jax.ShapeDtypeStruct((16, TAIL), bf16),
        in_specs=[pl.BlockSpec(memory_space=pl.ANY)],
        out_specs=pl.BlockSpec(memory_space=pl.ANY),
        scratch_shapes=[pltpu.SemaphoreType.DMA((2,))],
        compiler_params=pltpu.CompilerParams(
            collective_id=0, has_side_effects=True, vmem_limit_bytes=60 * 1024 * 1024
        ),
        name="heads",
    )(own)
    t = tables()
    constants = [
        t["scalars"], t["pw"], *t["g"], t["c2"], *t["a"], *t["b"], t["base"], t["gl"], *t["h"], t["cj"], *t["q"],
    ]
    constants = [jnp.asarray(c) for c in constants]
    anywhere = pl.BlockSpec(memory_space=pl.ANY)
    v = lambda shape, kind=f32: pltpu.VMEM(shape, kind)
    dma = pltpu.SemaphoreType.DMA
    out = pl.pallas_call(
        kernel,
        out_shape=jax.ShapeDtypeStruct((15, 128, 256), f32),
        in_specs=[anywhere] * (len(constants) + 3),
        out_specs=anywhere,
        scratch_shapes=[
            pltpu.SMEM((2, 640), f32), v((16, COLS), bf16), v((2, 16, 16, 8, 256)), v((2, 16, 16, 8, 256)),
            v((JC * 128, 512), bf16), v((JC * 128, 512), bf16), v((JC * 128, 512)),
            v((16, 16, 16, 256), bf16), v((16, 16, 16, 256), bf16),
            v((16, QC, 2, 2 * RQ, 128), bf16), v((QC, 16, 2, 2 * RQ, 128), bf16),
            v((8, 128)), v((16, 8, 128)), v((8, 128)), v((16, 8, 128)),
            v((512, 512), bf16), v((512, 512), bf16), v((2, 8, 256)),
            v((16, 256, 256), bf16), v((16, 256, 256), bf16), v((16, 256, 256), bf16), v((16, 256, 256), bf16),
            v((2, 128, 256)), v((2, 128, 128)),
            v((512, 512), bf16), v((512, 512), bf16), v((2, 256, 128)),
            v((512, 512), bf16), v((512, 512), bf16),
            v((16, 128, 256)), v((2, 16, 128, 256)),
            v((512, 2048)),
            v((16, 2, 2 * RQ, 128)), v((16, 2, 2 * RQ, 128)), v((15 * RQ, 512)), v((2, 15, RQ, 256)),
            dma((18,)), dma((16,)), dma((2,)), dma((2, 2)), dma, dma((NC,)), dma((NC,)), dma, dma((QC,)),
            dma((QC,)), dma((QC,)),
        ],
        compiler_params=pltpu.CompilerParams(
            collective_id=1, has_side_effects=True, vmem_limit_bytes=60 * 1024 * 1024
        ),
        name="dedisperse",
    )(own, tail, chirp_phase.reshape(128, 16, 256), *constants)
    return out.reshape(1, 15, 1, 128, 256)


def solution(mesh):
    return jax.shard_map(
        on_device,
        mesh=mesh,
        in_specs=(P("seg", "fft", None, None, None, None), P("fft", None, None, None)),
        out_specs=P("seg", None, "fft", None, None),
        check_vma=False,
    )
```

```python
import functools

import jax
import jax.numpy as jnp
import ml_dtypes
import numpy as np
from jax import lax
from jax.experimental import pallas as pl
from jax.experimental.pallas import tpu as pltpu
from jax.sharding import PartitionSpec as P

FFT_LEN = 8388608
LANES = 16
SEGS = 16
OWN = 61440
TAIL = 4096
COLS = OWN + TAIL
JC = 2
NC = 16 // JC
QC = 8
RQ = 16
KNEE = 4.0
POWER = 20
SHIFT = 2.0**-6.25
TINY = 1e-36

MESH = pl.DeviceIdType.MESH
f32 = jnp.float32
bf16 = jnp.bfloat16


def unit(numerator, modulus, direction):
    angle = (np.asarray(numerator, np.int64) % modulus) * (direction * 2.0 * np.pi / modulus)
    return np.cos(angle), np.sin(angle)


def halves(table):
    table = table.astype(np.float32)
    high = table.astype(ml_dtypes.bfloat16)
    low = (table - high.astype(np.float32)).astype(ml_dtypes.bfloat16)
    return high, low


@functools.lru_cache(maxsize=None)
def tables():
    n = FFT_LEN
    r16, r128, r256 = np.arange(16), np.arange(128), np.arange(256)
    out = {}
    c, s = unit(
        r16[None, :, None] * r16[None, None, :] * (n // 256) + r16[:, None, None] * r16[None, None, :],
        n,
        -1,
    )
    out["s1"] = np.stack([c, s]).astype(np.float32).reshape(2, -1)
    c, s = unit(r16[:, None] * r16[None, :], 256, 1)
    out["s2"] = np.stack([c, s])
    scalars = np.zeros((16, 2, 640), np.float32)
    scalars[:, :, :256] = out["s1"].reshape(2, 16, 256).transpose(1, 0, 2)
    scalars[:, :, 512:528] = out["s2"].transpose(1, 0, 2)
    out["scalars"] = scalars
    e = r16[:, None] + 16 * r16[None, :]
    ib = 16 * np.arange(8)[:, None] + 128 * r256[None, :]
    c, s = unit(e[:, :, None, None] * ib[None, None], n, -1)
    out["pw"] = np.stack([c, s]).astype(np.float32)
    c, s = unit(r256[:, None] * r256[None, :], 256, -1)
    out["g"] = halves(np.block([[c, s], [-s, c]]))
    res = r16[:, None] + 16 * np.arange(8)[None, :]
    c, s = unit(res[:, :, None] * r256[None, None, :], 32768, -1)
    out["c2"] = np.stack([c, s], axis=1).astype(np.float32)
    src, i = r16[:, None], np.arange(8)[None, :]
    num = (src + 16 * i)[None, None] * r128[None, :, None, None] * (n // 128)
    num = num + src[None, None] * 16 * r16[:, None, None, None]
    c, s = unit(num, n, -1)
    full = np.zeros((16, 2, 128, 16, 2, 8))
    full[:, 0, :, :, 0], full[:, 0, :, :, 1] = c, -s
    full[:, 1, :, :, 0], full[:, 1, :, :, 1] = s, c
    out["a"] = halves(full.reshape(16, 256, 256))
    num = r128[None, :, None] * r128[None, None, :] * (n // 128) + r128[None, :, None] * 16 * r16[:, None, None]
    c, s = unit(num, n, 1)
    out["b"] = halves(np.concatenate([np.concatenate([c, -s], 2), np.concatenate([s, c], 2)], 1))
    c, s = unit(r128[:, None] * r256[None, :], 32768, 1)
    out["base"] = np.stack([c, s]).astype(np.float32)
    c, s = unit(r16[:, None] * r128[None, :], n, 1)
    gl = np.stack([c, s], axis=1).astype(np.float32)
    out["gl"] = np.ascontiguousarray(np.broadcast_to(gl[..., None], gl.shape + (128,)))
    q, par, jj = np.meshgrid(np.arange(QC), np.arange(2), np.arange(RQ), indexing="ij")
    hh = 2 * (RQ * q + jj) + par
    hh = hh.reshape(QC, 2 * RQ)
    c, s = unit(hh[:, :, None] * r256[None, None, :], 256, 1)
    both = np.concatenate([np.concatenate([c, -s], 2), np.concatenate([s, c], 2)], 1)
    out["h"] = halves(both.reshape(512, 512))
    e = r16[:, None] + 16 * r16[None, :]
    c, s = unit(hh.reshape(1, 256, 1) * e[:, None, :], 65536, 1)
    cj = np.zeros((16, 2, 256, 128), np.float32)
    cj[:, 0, :, :16], cj[:, 1, :, :16] = c, s
    out["cj"] = cj
    r = np.arange(256)
    c, s = unit(r[:, None] * r256[None, :], 256, -1)
    out["q"] = halves(np.block([[c, s], [-s, c]]) * 2.0**-27)
    return out


def cmul(ar, ai, br, bi):
    return ar * br - ai * bi, ar * bi + ai * br


def radix4(x, sign):
    (ar, ai), (br, bi), (cr, ci), (dr, di) = x
    pr, pi, mr, mi = ar + cr, ai + ci, ar - cr, ai - ci
    qr, qi, nr, ni = br + dr, bi + di, br - dr, bi - di
    if sign > 0:
        ur, ui = -ni, nr
        return [(pr + qr, pi + qi), (mr - ni, mi + nr), (pr - qr, pi - qi), (mr + ni, mi - nr)]
    return [(pr + qr, pi + qi), (mr + ni, mi - nr), (pr - qr, pi - qi), (mr - ni, mi + nr)]


def turn(x, power, sign):
    xr, xi = x
    power = power % 16
    if power == 0:
        return x
    if power == 4:
        return (-xi, xr) if sign > 0 else (xi, -xr)
    root = float(np.sqrt(0.5))
    if power == 2:
        return ((xr - xi) * root, (xr + xi) * root) if sign > 0 else ((xr + xi) * root, (xi - xr) * root)
    if power == 6:
        return ((-xr - xi) * root, (xr - xi) * root) if sign > 0 else ((xi - xr) * root, (-xr - xi) * root)
    c = float(np.cos(2 * np.pi * power / 16))
    s = float(sign * np.sin(2 * np.pi * power / 16))
    return (xr * c - xi * s, xr * s + xi * c)


def radix16(x, sign):
    inner = [radix4([x[4 * n1 + n2] for n1 in range(4)], sign) for n2 in range(4)]
    out = [None] * 16
    for k1 in range(4):
        column = radix4([turn(inner[n2][k1], n2 * k1, sign) for n2 in range(4)], sign)
        for k2 in range(4):
            out[k1 + 4 * k2] = column[k2]
    return out


def split(x):
    high = x.astype(bf16)
    return high, (x - high.astype(f32)).astype(bf16)


def dot(a, b):
    return lax.dot_general(a, b, (((1,), (0,)), ((), ())), preferred_element_type=f32)


def dot3(ah, al, bh, bl):
    return dot(ah, bh) + dot(al, bh) + dot(ah, bl)


def encode(x, inverse):
    a = jnp.abs(x) * inverse
    v = a * a + 1.0
    w = (a + v * lax.rsqrt(v)) * SHIFT
    w2 = w * w
    w4 = w2 * w2
    w8 = w4 * w4
    y = (w8 * w8) * w4
    return jnp.where(x < 0, -y, y)


def decode(y, half_scale):
    t = jnp.log(jnp.abs(y)) * (1.0 / POWER) + float(-np.log(SHIFT))
    w = jnp.exp(t)
    a = (w - jnp.exp(-t)) * half_scale
    return jnp.where(y < 0, -a, a)


def cos_sin(x):
    y = x * 0.5
    z = y * y
    s = 1.0 / 6227020800.0
    for factor in (-1.0 / 39916800.0, 1.0 / 362880.0, -1.0 / 5040.0, 1.0 / 120.0, -1.0 / 6.0, 1.0):
        s = s * z + factor
    s = s * y
    c = 1.0 / 479001600.0
    for factor in (-1.0 / 3628800.0, 1.0 / 40320.0, -1.0 / 720.0, 1.0 / 24.0, -0.5, 1.0):
        c = c * z + factor
    return 1.0 - 2.0 * s * s, 2.0 * s * c


def aligned(index, size):
    return pl.ds(pl.multiple_of(index * size, size), size)


def head_kernel(x_hbm, tail_hbm, sems):
    seg = lax.axis_index("seg")
    phase = lax.rem(seg, 4)
    before, after = lax.rem(seg + SEGS - 1, SEGS), lax.rem(seg + 1, SEGS)
    barrier = pltpu.get_barrier_semaphore()
    head = pltpu.make_async_remote_copy(
        src_ref=x_hbm.at[:, pl.ds(0, TAIL)], dst_ref=tail_hbm, send_sem=sems.at[0], recv_sem=sems.at[1],
        device_id={"seg": before}, device_id_type=MESH,
    )

    @pl.when(phase != 3)
    def _():
        pl.semaphore_signal(barrier, inc=1, device_id={"seg": after}, device_id_type=MESH)

    @pl.when(phase != 0)
    def _():
        pl.semaphore_wait(barrier, 1)
        head.start()

    @pl.when(phase != 3)
    def _():
        head.wait_recv()

    @pl.when(phase != 0)
    def _():
        head.wait_send()


def kernel(
    x_hbm, tail_hbm, chirp_hbm, scalars_hbm, pw_hbm, gh_hbm, gl_hbm, c2_hbm, ah_hbm, al_hbm, bh_hbm, bl_hbm,
    base_hbm, lane_hbm, hh_hbm, hl_hbm, cj_hbm, qh_hbm, ql_hbm,
    out_hbm,
    scalars, x_v, d_v, pw_v, lhs_h, lhs_l, y_v, send1, recv1, send2, recv2, scale1_out, scale1, scale2_out, scale2,
    gh_v, gl_v, c2_v, ah_v, al_v, bh_v, bl_v, base_v, lane_v, hh_v, hl_v, cj_v, qh_v, ql_v,
    chirp_v, turn_v, u_v, v_v, z_v, xl_v, stage,
    load_sem, chirp_sem, head_sems, scale_sems, send_sem1, recv_sem1, own_sem1, send_sem2, recv_sem2, own_sem2,
    out_sem,
):
    lane = lax.axis_index("fft")
    seg = lax.axis_index("seg")
    lane_x, lane_z = lane // 4, lax.rem(lane, 4)

    def peer(turn_index):
        step_z, step_x = (2, 1, 3, 0)[turn_index // 4], (turn_index + 1) % 4
        return lax.rem(lane_x + step_x, 4) * 4 + lax.rem(lane_z + step_z, 4)

    phase = lax.rem(seg, 4)
    before, after = lax.rem(seg + SEGS - 1, SEGS), lax.rem(seg + 1, SEGS)

    def load(source, target, index):
        copy = pltpu.make_async_copy(source, target, load_sem.at[index])
        copy.start()
        return copy

    load_x = load(x_hbm, x_v.at[:, pl.ds(0, OWN)], 0)

    barrier = pltpu.get_barrier_semaphore()

    @pl.when((phase == 3) & (seg < SEGS - 1))
    def _():
        pl.semaphore_signal(barrier, inc=1, device_id={"seg": after}, device_id_type=MESH)

    for s in range(LANES - 1):
        pl.semaphore_signal(barrier, inc=1, device_id={"fft": peer(s)}, device_id_type=MESH)
    load_tail = pltpu.make_async_copy(tail_hbm, x_v.at[:, pl.ds(OWN, TAIL)], load_sem.at[17])
    pl.when(phase != 3)(load_tail.start)
    load_scalars = load(scalars_hbm.at[lane], scalars, 16)
    load_pw = load(pw_hbm, pw_v, 1)
    load_g = [load(gh_hbm, gh_v, 2), load(gl_hbm, gl_v, 3), load(c2_hbm.at[lane], c2_v, 4)]
    piece = TAIL // 4
    heads = [
        pltpu.make_async_remote_copy(
            src_ref=x_hbm.at[:, pl.ds(h * piece, piece)], dst_ref=x_v.at[:, pl.ds(OWN + h * piece, piece)],
            send_sem=head_sems.at[0, h], recv_sem=head_sems.at[1, h],
            device_id={"seg": before}, device_id_type=MESH,
        )
        for h in range(4)
    ]
    load_x.wait()
    load_scalars.wait()
    pl.when(phase != 3)(load_tail.wait)

    @pl.when(seg == SEGS - 1)
    def _():
        x_v[:, pl.ds(OWN, TAIL)] = jnp.zeros((16, TAIL), bf16)

    late = [
        load(ah_hbm, ah_v, 5), load(al_hbm, al_v, 6), load(bh_hbm, bh_v, 7), load(bl_hbm, bl_v, 8),
        load(base_hbm, base_v, 9), load(lane_hbm.at[lane], lane_v, 10), load(hh_hbm, hh_v, 11),
        load(hl_hbm, hl_v, 12), load(cj_hbm.at[lane], cj_v, 13), load(qh_hbm, qh_v, 14), load(ql_hbm, ql_v, 15),
    ]

    def chirp_copy(j):
        return pltpu.make_async_copy(chirp_hbm.at[:, j, :], chirp_v.at[j], chirp_sem.at[j])

    def chirp_start(j, carry):
        chirp_copy(j).start()
        return carry

    lax.fori_loop(0, 16, chirp_start, 0)

    def first_pass(t, energy):
        a_lo, half = t // 2, lax.rem(t, 2)
        x = []
        for a_hi in range(16):
            block = x_v[:, aligned((16 * a_hi + a_lo) * 2 + half, 128)].astype(f32)
            re, im = block[:8], block[8:]
            energy = energy + (re * re + im * im)
            x.append((re, im))
        x = radix16(x, -1)
        for e_lo in range(16):
            where = a_lo * 16 + e_lo
            re, im = cmul(*x[e_lo], scalars[0, where], scalars[1, where])
            d_v[0, e_lo, a_lo, :, aligned(half, 128)] = re
            d_v[1, e_lo, a_lo, :, aligned(half, 128)] = im
        return energy

    energy = jnp.zeros((8, 128), f32)
    for h in range(4):
        pl.when((phase == 3) & (seg < SEGS - 1))(heads[h].wait_recv)
        energy = lax.fori_loop(8 * h, 8 * h + 8, first_pass, energy)

    def scale_of(energy):
        total = jnp.sum(jnp.sum(energy, axis=1, keepdims=True), axis=0, keepdims=True)
        mean = jnp.maximum(jnp.broadcast_to(total, (8, 128)), TINY)
        return mean * lax.rsqrt(mean) * (1.0 / KNEE)

    def send_scale(value, out_ref, in_ref, sems):
        out_ref[...] = value
        in_ref[lane] = value

        for s in range(LANES - 1):
            pltpu.make_async_remote_copy(
                src_ref=out_ref, dst_ref=in_ref.at[lane], send_sem=sems.at[0], recv_sem=sems.at[1],
                device_id={"fft": peer(s)}, device_id_type=MESH,
            ).start()

    def wait_total(ref, sem):
        pltpu.make_async_copy(ref, ref, sem).wait()

    my_scale = scale_of(energy * 0.125)
    inverse = 1.0 / my_scale
    inverse = jnp.concatenate([inverse, inverse], axis=1)

    load_pw.wait()

    def second_pass(t, carry):
        e_lo, half = t // 2, lax.rem(t, 2)
        cols = aligned(half, 128)
        x = [(d_v[0, e_lo, a_lo, :, cols], d_v[1, e_lo, a_lo, :, cols]) for a_lo in range(16)]
        x = radix16(x, -1)
        for e_hi in range(16):
            re, im = cmul(*x[e_hi], pw_v[0, e_lo, e_hi, :, cols], pw_v[1, e_lo, e_hi, :, cols])
            d_v[0, e_lo, e_hi, :, cols] = re
            d_v[1, e_lo, e_hi, :, cols] = im
        return carry

    lax.fori_loop(0, 32, second_pass, 0)

    for copy in load_g:
        copy.wait()

    @pl.when((phase == 0) & (seg > 0))
    def _():
        pl.semaphore_wait(barrier, LANES)
        for head in heads:
            head.start()

    @pl.when((phase != 0) | (seg == 0))
    def _():
        pl.semaphore_wait(barrier, LANES - 1)

    send_scale(my_scale, scale1_out, scale1, scale_sems.at[0])

    def chunk1(ref, jc, s):
        return ref.at[peer(s), pl.ds(jc * JC, JC)]

    def landing1(jc, source):
        return recv1.at[pl.ds(jc * JC, JC), source]

    rows = JC * 8

    def transform_b(jc, carry):
        for u in range(LANES):
            dest = peer(u)
            re = d_v[0, dest, pl.ds(jc * JC, JC)].reshape(rows, 256)
            im = d_v[1, dest, pl.ds(jc * JC, JC)].reshape(rows, 256)
            high, low = split(jnp.concatenate([re, im], axis=1))
            lhs_h[pl.ds(u * rows, rows), :] = high
            lhs_l[pl.ds(u * rows, rows), :] = low
        y_v[...] = dot3(lhs_h[...], lhs_l[...], gh_v[...], gl_v[...])
        cr, ci = c2_v[0][None], c2_v[1][None]
        for u in range(LANES):
            dest = peer(u)
            block = y_v[pl.ds(u * rows, rows), :]
            re = block[:, :256].reshape(JC, 8, 256)
            im = block[:, 256:].reshape(JC, 8, 256)
            re, im = cmul(re, im, cr, ci)
            coded = jnp.concatenate([encode(re, inverse[None]), encode(im, inverse[None])], axis=1)
            send1[dest, pl.ds(jc * JC, JC)] = coded.astype(bf16)
            if u < LANES - 1:
                pltpu.make_async_remote_copy(
                    src_ref=chunk1(send1, jc, u), dst_ref=landing1(jc, lane),
                    send_sem=send_sem1, recv_sem=recv_sem1.at[jc],
                    device_id={"fft": dest}, device_id_type=MESH,
                ).start()
            else:
                pltpu.make_async_copy(chunk1(send1, jc, u), landing1(jc, lane), own_sem1.at[jc]).start()
        return carry

    lax.fori_loop(0, NC, transform_b, 0)

    def response(j, carry):
        chirp_copy(j).wait()
        c, s = cos_sin(chirp_v[j])
        turn_v[0, j] = c
        turn_v[1, j] = s
        return carry

    lax.fori_loop(0, 16, response, 0)
    for copy in late:
        copy.wait()
    for part in range(2):
        cols = pl.ds(part * 128, 128)
        re, im = cmul(base_v[0, :, cols], base_v[1, :, cols], lane_v[0], lane_v[1])
        base_v[0, :, cols] = re
        base_v[1, :, cols] = im

    wait_total(scale1.at[pl.ds(0, LANES - 1)], scale_sems.at[0, 1])

    def middle(j):
        half_scale = (scale1[...] * 0.5)[:, 0:1, :]
        half_scale = jnp.concatenate([half_scale, half_scale], axis=2)
        z = decode(recv1[j].astype(f32), half_scale).reshape(256, 256)
        zh, zl = split(z)
        o = dot3(ah_v[j], al_v[j], zh, zl)
        re, im = cmul(o[:128], o[128:], turn_v[0, j], turn_v[1, j])
        ph, pll = split(jnp.concatenate([re, im], axis=0))
        o = dot3(bh_v[j], bl_v[j], ph, pll)
        re, im = cmul(o[:128], o[128:], base_v[0], base_v[1])
        power = jnp.sum((re * re + im * im).reshape(16, 8, 256), axis=0)
        return jnp.concatenate([re.T, im.T], axis=0), power

    def middle_chunk(jc, energy):
        wait_total(recv1.at[pl.ds(jc * JC, JC), pl.ds(0, LANES - 1)], recv_sem1.at[jc])
        wait_total(landing1(jc, lane), own_sem1.at[jc])
        parts = []
        for r in range(JC):
            part, power = middle(jc * JC + r)
            parts.append(part)
            energy = energy + power
        high, low = split(jnp.concatenate(parts, axis=1))
        u_v[:, aligned(jc, JC * 128)] = dot3(hh_v[...], hl_v[...], high, low)
        return energy

    energy = lax.fori_loop(0, NC, middle_chunk, jnp.zeros((8, 256), f32))
    my_scale = scale_of((energy[:, :128] + energy[:, 128:]) * (1.0 / 128.0))
    send_scale(my_scale, scale2_out, scale2, scale_sems.at[1])
    inverse2 = (1.0 / my_scale)[0:1, :]

    def post(q, carry):
        def rows_of(rt, inner):
            top = aligned(rt, 8)
            high = pl.ds(pl.multiple_of(q * 4 * RQ + rt * 8, 8), 8)
            low = pl.ds(pl.multiple_of(q * 4 * RQ + 2 * RQ + rt * 8, 8), 8)
            table = pl.ds(pl.multiple_of(q * 2 * RQ + rt * 8, 8), 8)
            tr, ti = cj_v[0, table, :], cj_v[1, table, :]
            x = []
            for j in range(16):
                cols = pl.ds(j * 128, 128)
                x.append(cmul(u_v[high, cols], u_v[low, cols], tr[:, j : j + 1], ti[:, j : j + 1]))
            x = radix16(x, 1)
            for l in range(16):
                re, im = cmul(*x[l], scalars[0, 512 + l], scalars[1, 512 + l])
                v_v[l, 0, top, :] = re
                v_v[l, 1, top, :] = im
            return inner

        lax.fori_loop(0, 2 * RQ // 8, rows_of, 0)

        for s in range(LANES):
            dest = peer(s)
            send2[dest, q] = encode(v_v[dest], inverse2[None]).astype(bf16)
            if s < LANES - 1:
                pltpu.make_async_remote_copy(
                    src_ref=send2.at[dest, q], dst_ref=recv2.at[q, lane],
                    send_sem=send_sem2, recv_sem=recv_sem2.at[q],
                    device_id={"fft": dest}, device_id_type=MESH,
                ).start()
            else:
                pltpu.make_async_copy(send2.at[dest, q], recv2.at[q, lane], own_sem2.at[q]).start()
        return carry

    lax.fori_loop(0, QC, post, 0)

    wait_total(scale2.at[pl.ds(0, LANES - 1)], scale_sems.at[1, 1])

    def out_copy(q):
        return pltpu.make_async_copy(stage.at[lax.rem(q, 2)], out_hbm.at[:, pl.ds(q * RQ, RQ), :], out_sem.at[q])

    def final(q, carry):
        wait_total(recv2.at[q, pl.ds(0, LANES - 1)], recv_sem2.at[q])
        wait_total(recv2.at[q, lane], own_sem2.at[q])

        def undo(source, inner):
            half_scale = (scale2[source] * 0.5)[0:1, :]
            z_v[source] = decode(recv2[q, source].astype(f32), half_scale[None])
            return inner

        lax.fori_loop(0, LANES, undo, 0)

        def rows_of(rt, inner):
            top = aligned(rt, 8)
            par, jt = rt // (RQ // 8), lax.rem(rt, RQ // 8)
            x = radix16([(z_v[s, 0, top, :], z_v[s, 1, top, :]) for s in range(16)], 1)
            for t in range(15):
                where = pl.ds(pl.multiple_of(t * RQ + jt * 8, 8), 8)
                xl_v[where, aligned(par, 128)] = x[t][0]
                xl_v[where, aligned(par + 2, 128)] = x[t][1]
            return inner

        lax.fori_loop(0, 2 * RQ // 8, rows_of, 0)

        @pl.when(q >= 2)
        def _():
            out_copy(q - 2).wait()

        high, low = split(xl_v[...])
        y = dot3(high, low, qh_v[...], ql_v[...])
        re, im = y[:, :256], y[:, 256:]
        stage[lax.rem(q, 2)] = (re * re + im * im).reshape(15, RQ, 256)
        out_copy(q).start()
        return carry

    lax.fori_loop(0, QC, final, 0)
    out_copy(QC - 2).wait()
    out_copy(QC - 1).wait()

    @pl.when((phase == 0) & (seg > 0))
    def _():
        for head in heads:
            head.wait_send()

    wait_total(scale1.at[pl.ds(0, LANES - 1)], scale_sems.at[0, 0])
    wait_total(scale2.at[pl.ds(0, LANES - 1)], scale_sems.at[1, 0])
    wait_total(send1.at[pl.ds(0, LANES - 1)], send_sem1)
    wait_total(send2.at[pl.ds(0, LANES - 1)], send_sem2)


def on_device(baseband, chirp_phase):
    own = baseband.reshape(16, OWN)
    tail = pl.pallas_call(
        head_kernel,
        out_shape=jax.ShapeDtypeStruct((16, TAIL), bf16),
        in_specs=[pl.BlockSpec(memory_space=pl.ANY)],
        out_specs=pl.BlockSpec(memory_space=pl.ANY),
        scratch_shapes=[pltpu.SemaphoreType.DMA((2,))],
        compiler_params=pltpu.CompilerParams(
            collective_id=0, has_side_effects=True, vmem_limit_bytes=60 * 1024 * 1024
        ),
        name="heads",
    )(own)
    t = tables()
    constants = [
        t["scalars"], t["pw"], *t["g"], t["c2"], *t["a"], *t["b"], t["base"], t["gl"], *t["h"], t["cj"], *t["q"],
    ]
    constants = [jnp.asarray(c) for c in constants]
    anywhere = pl.BlockSpec(memory_space=pl.ANY)
    v = lambda shape, kind=f32: pltpu.VMEM(shape, kind)
    dma = pltpu.SemaphoreType.DMA
    out = pl.pallas_call(
        kernel,
        out_shape=jax.ShapeDtypeStruct((15, 128, 256), f32),
        in_specs=[anywhere] * (len(constants) + 3),
        out_specs=anywhere,
        scratch_shapes=[
            pltpu.SMEM((2, 640), f32), v((16, COLS), bf16), v((2, 16, 16, 8, 256)), v((2, 16, 16, 8, 256)),
            v((JC * 128, 512), bf16), v((JC * 128, 512), bf16), v((JC * 128, 512)),
            v((16, 16, 16, 256), bf16), v((16, 16, 16, 256), bf16),
            v((16, QC, 2, 2 * RQ, 128), bf16), v((QC, 16, 2, 2 * RQ, 128), bf16),
            v((8, 128)), v((16, 8, 128)), v((8, 128)), v((16, 8, 128)),
            v((512, 512), bf16), v((512, 512), bf16), v((2, 8, 256)),
            v((16, 256, 256), bf16), v((16, 256, 256), bf16), v((16, 256, 256), bf16), v((16, 256, 256), bf16),
            v((2, 128, 256)), v((2, 128, 128)),
            v((512, 512), bf16), v((512, 512), bf16), v((2, 256, 128)),
            v((512, 512), bf16), v((512, 512), bf16),
            v((16, 128, 256)), v((2, 16, 128, 256)),
            v((512, 2048)),
            v((16, 2, 2 * RQ, 128)), v((16, 2, 2 * RQ, 128)), v((15 * RQ, 512)), v((2, 15, RQ, 256)),
            dma((18,)), dma((16,)), dma((2, 4)), dma((2, 2)), dma, dma((NC,)), dma((NC,)), dma, dma((QC,)),
            dma((QC,)), dma((QC,)),
        ],
        compiler_params=pltpu.CompilerParams(
            collective_id=1, has_side_effects=True, vmem_limit_bytes=60 * 1024 * 1024
        ),
        name="dedisperse",
    )(own, tail, chirp_phase.reshape(128, 16, 256), *constants)
    return out.reshape(1, 15, 1, 128, 256)


def solution(mesh):
    return jax.shard_map(
        on_device,
        mesh=mesh,
        in_specs=(P("seg", "fft", None, None, None, None), P("fft", None, None, None)),
        out_specs=P("seg", None, "fft", None, None),
        check_vma=False,
    )
```
